128 devices in a mesh: ctx: 32 (over y, x, core), head: 4 (over z).
Axes of the slice: x: 4, y: 4, z: 4, core: 2. Of those that a mesh axis runs over, the one named last changes fastest.
Arguments:
- prefix: bfloat16 [262144, 1024], P(('ctx', 'head')), may hold values from -6 to 6
- keep_blocks: int32 [4, 32, 16], P('head', 'ctx'), may hold values from 0 to 15, each once within a row
- keep_count: int32 [4, 32], P('head', 'ctx'), may hold values from 1 to 16, 256 in all within a row
- latent_inputs: bfloat16 [512, 1024], P('ctx'), may hold values from -6 to 6
- latent_pos: int32 [512], replicated, may hold values from 0 to 262143
- w_query: bfloat16 [1024, 1024], P(None, 'head')
- w_key: bfloat16 [1024, 1024], replicated, may hold values from -0.1875 to 0.1875
- w_value: bfloat16 [1024, 1024], replicated, may hold values from -0.1875 to 0.1875
Outputs:
- attended: bfloat16 [512, 1024], P('ctx', 'head')
The draws below stay inside these ranges and needn't reach their ends.
Inputs may be any that keep to these rules, and one draw needn't show every extreme that they name: keep_blocks[h, c, :] lists each of the 16 block numbers once; the first keep_count[h, c] entries are the kept blocks. For every index h, keep_count[h, :] sums to 256, and its largest entry is 16.
All inputs are finite; a program needn't handle non-finite values. No bound on the sum of `keep_count` on one device may be relied on, other than what follows from the above.
Results may differ from the reference program's by a relative error of at most 0.0085.
The reference program's roundings to bfloat16 on the way count: a program that leaves them out, or rounds other values in their place, can miss the bound.
Values may be sent and summed in bfloat16 or wider, within the bound.
A program may use at most 128 MiB of HBM per device.

```python
import math
import jax
import jax.numpy as jnp
import numpy as np
from jax import lax

D = 1024
HEADS = 16
HD = 64
BLOCK = 128
BLK_DEV = 16
LAT_DEV = 16
ROWS = 262144
LAT = 512
N_CTX = 32
N_HEAD = 4


def draw_w_query(key, part):
    raw_weights = jax.random.normal(key, (D, HEADS * HD), jnp.float32) * D ** (-0.5)
    return raw_weights.astype(jnp.bfloat16)


def plant(result, rng, low, largest):
    dims = result.shape
    spot = [jax.random.randint(jax.random.fold_in(rng, axis), (), 0, dims[axis]) for axis in range(len(dims))]
    result = result.at[tuple(spot)].set(low)
    longest = dims.index(max(dims))
    spot[longest] = (spot[longest] + 1) % dims[longest]
    return result.at[tuple(spot)].set(largest)


def level_of(rng, extent, cuts, smallest, high):
    gain, own = 1.0, jax.random.fold_in(rng, 6)
    for position, parts in cuts:
        heights = jnp.exp(jax.random.uniform(jax.random.fold_in(own, position), (parts,), jnp.float32, smallest / len(cuts), high / len(cuts)))
        gain = gain * jnp.repeat(heights, extent[position] // parts).reshape([-1 if axis == position else 1 for axis in range(len(extent))])
    return gain


def length_profile(number_of, total, bound, skew):
    portions = [(1 << 20) // math.isqrt(grade ** skew) + 1 for grade in range(2, number_of + 1)]
    rest, counts = total - bound - (number_of - 1), [1] * (number_of - 1)
    while rest > 0:
        candidates = [i for i in range(number_of - 1) if counts[i] < bound]
        mass, budget = sum([portions[i] for i in candidates]), rest
        for i in candidates:
            more = min(bound - counts[i], max(1, budget * portions[i] // mass), rest)
            counts[i] = counts[i] + more
            rest = rest - more
    return np.array([bound] + counts)


def uneven(key, count, total, bound, lean):
    if count == 2:
        one = jax.random.randint(key, (), max(1, total - bound), min(bound, total - 1) + 1)
        return jnp.stack([one, total - one])
    sizes = jnp.asarray(length_profile(count, total, bound, lean), jnp.int32)
    pairs = (count - 1) // 2
    source_of, sink = sizes[1:1 + 2 * pairs:2], sizes[2:2 + 2 * pairs:2]
    slack = jnp.minimum(source_of - 1, bound - sink)
    moved = jax.random.randint(jax.random.fold_in(key, 1), (pairs,), 0, 1 << 20) % (slack + 1)
    sizes = sizes.at[1:1 + 2 * pairs:2].set(source_of - moved).at[2:2 + 2 * pairs:2].set(sink + moved)
    return sizes[jax.random.permutation(jax.random.fold_in(key, 2), count)]


def bell_draw(own_key, shape, width, bound, pieces=(), kind=jnp.bfloat16):
    values = jax.random.normal(own_key, shape, jnp.float32) * width
    if len(pieces) > 0:
        values = level_of(own_key, shape, pieces, -0.22, 0.18) * values
    return jnp.clip(values, min=-bound, max=bound).astype(kind)


def setup_inputs(seed: int = 0) -> dict:
    key_list = jax.random.split(jax.random.key(seed), 9)
    return {
        "prefix": bell_draw(key_list[0], (ROWS, D), 1.0, 6.0, ((0, 128),)),
        "keep_blocks": jax.vmap(lambda own: jax.random.permutation(own, BLK_DEV))(jax.random.split(key_list[1], N_HEAD * N_CTX)).reshape((N_HEAD, N_CTX, BLK_DEV)).astype(jnp.int32),
        "keep_count": jax.vmap(lambda own: uneven(own, N_CTX, N_CTX * (BLK_DEV // 2), BLK_DEV, 2))(jax.random.split(key_list[2], N_HEAD)).reshape((N_HEAD, N_CTX)).astype(jnp.int32),
        "latent_inputs": bell_draw(key_list[3], (LAT, D), 1.0, 6.0, ((0, 32),)),
        "latent_pos": plant(jax.random.randint(key_list[4], (LAT,), 0, ROWS), jax.random.fold_in(key_list[4], 1), 0, ROWS - 1).astype(jnp.int32),
        "w_query": draw_w_query(jax.random.fold_in(key_list[8], 71), 0),
        "w_key": bell_draw(key_list[6], (D, HEADS * HD), D ** -0.5, 0.1875),
        "w_value": bell_draw(key_list[7], (D, HEADS * HD), D ** -0.5, 0.1875),
    }


NEG_FILL = -1e+30
EPSILON = 1e-06

def normalize(source_rows):
    wide_rows = source_rows.astype(jnp.float32)
    factor = lax.rsqrt(lax.optimization_barrier(jnp.mean(wide_rows * wide_rows, axis=-1, keepdims=True)) + EPSILON)
    return (wide_rows * factor).astype(jnp.bfloat16)

def reference(prefix, keep_blocks, keep_count, latent_inputs, latent_pos, w_query, w_key, w_value):
    latents = LAT_DEV * N_CTX
    order_ids = jnp.arange(BLK_DEV, dtype=jnp.int32)
    matched = (keep_blocks[:, :, :, None] == order_ids[None, None, None, :]) & (order_ids[None, None, :, None] < keep_count[:, :, None, None])
    kept_grid = jnp.any(matched, axis=2)
    kept_flat = jnp.transpose(kept_grid, (1, 0, 2)).reshape(-1)
    kept_total = N_CTX * N_HEAD * (BLK_DEV // 2)
    block_ids = jnp.nonzero(kept_flat, size=kept_total)[0].astype(jnp.int32)
    all_blocks = prefix.reshape(N_CTX * N_HEAD * BLK_DEV, BLOCK, D)
    kept_rows = jnp.take(all_blocks, block_ids, axis=0).reshape(kept_total * BLOCK, D)
    key_pos = (block_ids[:, None] * BLOCK + jnp.arange(BLOCK, dtype=jnp.int32)[None, :]).reshape(-1)
    normed = normalize(kept_rows)
    key_all = jnp.dot(normed, w_key, preferred_element_type=jnp.float32).astype(jnp.bfloat16)
    value_all = jnp.dot(normed, w_value, preferred_element_type=jnp.float32).astype(jnp.bfloat16)
    latent_normed = normalize(latent_inputs)
    query = (jnp.dot(latent_normed, w_query, preferred_element_type=jnp.float32) * HD ** (-0.5)).astype(jnp.bfloat16)
    self_key = jnp.dot(latent_normed, w_key, preferred_element_type=jnp.float32).astype(jnp.bfloat16)
    self_value = jnp.dot(latent_normed, w_value, preferred_element_type=jnp.float32).astype(jnp.bfloat16)
    self_score = lax.optimization_barrier(jnp.sum((query.astype(jnp.float32) * self_key.astype(jnp.float32)).reshape(latents, HEADS, HD), axis=2))
    block_rows = min(512, latents)
    block_count = latents // block_rows
    key_count = kept_total * BLOCK
    key_heads = key_all.reshape(key_count, HEADS, HD).transpose(1, 0, 2)
    value_heads = value_all.reshape(key_count, HEADS, HD).transpose(1, 0, 2)
    query_heads = query.reshape(block_count, block_rows, HEADS, HD).transpose(2, 0, 1, 3)
    self_scores = self_score.reshape(block_count, block_rows, HEADS).transpose(2, 0, 1)
    self_values = self_value.reshape(block_count, block_rows, HEADS, HD).transpose(2, 0, 1, 3)
    pos_blocks = latent_pos.reshape(block_count, block_rows)

    def per_head(head_args):
        key_head, value_head, query_head, score_head, svalue_head = head_args

        def per_block(block_args):
            query_block, pos_block, sscore_block, svalue_block = block_args
            scores = jnp.dot(query_block, key_head.T, preferred_element_type=jnp.float32)
            allowed = key_pos[None, :] < pos_block[:, None]
            masked = jnp.where(allowed, scores, NEG_FILL)
            row_top = jnp.maximum(lax.optimization_barrier(jnp.max(masked, axis=1)), sscore_block)
            weights = jnp.where(allowed, jnp.exp(masked - row_top[:, None]), 0.0)
            self_weight = jnp.exp(sscore_block - row_top)
            denominator = lax.optimization_barrier(jnp.sum(weights, axis=1)) + self_weight
            numerator = jnp.dot(weights.astype(jnp.bfloat16), value_head, preferred_element_type=jnp.float32)
            numerator = numerator + self_weight[:, None] * svalue_block.astype(jnp.float32)
            return (numerator / denominator[:, None]).astype(jnp.bfloat16)
        return lax.map(per_block, (query_head, pos_blocks, score_head, svalue_head))
    results = lax.map(per_head, (key_heads, value_heads, query_heads, self_scores, self_values))
    return results.transpose(1, 2, 0, 3).reshape(latents, HEADS * HD)
```

```python
import functools

import jax
import jax.numpy as jnp
from jax import lax
from jax.experimental import pallas as pl
from jax.experimental.pallas import tpu as pltpu
from jax.sharding import PartitionSpec as P

HD = 64
BLOCK = 128
EPSILON = 1e-06
NEG_FILL = -1e30
FAR = 1 << 30
AXES = ("ctx", "head")
F32, BF16 = jnp.float32, jnp.bfloat16


def normed(rows):
    wide = rows.astype(F32)
    factor = lax.rsqrt(jnp.mean(wide * wide, axis=-1, keepdims=True) + EPSILON)
    return (wide * factor).astype(BF16)


def dot(a, b):
    return jnp.dot(a, b, preferred_element_type=F32)


def pick_dot(x, ones):
    first = x.astype(BF16)
    rest = x - first.astype(F32)
    second = rest.astype(BF16)
    third = (rest - second.astype(F32)).astype(BF16)
    ones = ones.astype(BF16)
    return dot(first, ones) + dot(second, ones) + dot(third, ones)


def iota(shape, dim):
    return lax.broadcasted_iota(jnp.int32, shape, dim)


def split_two(x):
    high = x.astype(BF16).astype(F32)
    return high, x - high


def latent_kernel(head_ref, lat_ref, wq_ref, wk_ref, wv_ref, q_ref, sv_ref, ss_ref):
    n = normed(lat_ref[...])
    q = (dot(n, wq_ref[...]) * HD ** (-0.5)).astype(BF16)
    k = dot(n, wk_ref[...]).astype(BF16)
    q_ref[...] = q
    sv_ref[...] = dot(n, wv_ref[...]).astype(BF16)
    prod = q.astype(F32) * k.astype(F32)
    width = prod.shape[1]
    heads = width // HD
    pick = (iota((width, 128), 0) // HD == iota((width, 128), 1) % heads).astype(F32)
    ss_ref[...] = pick_dot(prod, pick)


def latent_part(head, latents, w_query, w_key, w_value):
    rows, d = latents.shape
    width = w_query.shape[1]
    whole = lambda i, h: (0, 0)
    mine = lambda i, h: (0, h[0])
    return pl.pallas_call(
        latent_kernel,
        grid_spec=pltpu.PrefetchScalarGridSpec(
            num_scalar_prefetch=1,
            grid=(1,),
            in_specs=[
                pl.BlockSpec((rows, d), whole),
                pl.BlockSpec((d, width), whole),
                pl.BlockSpec((d, width), mine),
                pl.BlockSpec((d, width), mine),
            ],
            out_specs=[
                pl.BlockSpec((rows, width), whole),
                pl.BlockSpec((rows, width), whole),
                pl.BlockSpec((rows, 128), whole),
            ],
        ),
        out_shape=[
            jax.ShapeDtypeStruct((rows, width), BF16),
            jax.ShapeDtypeStruct((rows, width), BF16),
            jax.ShapeDtypeStruct((rows, 128), F32),
        ],
        name="latent_part",
        cost_estimate=pl.CostEstimate(flops=6 * rows * d * width, bytes_accessed=6 * d * width, transcendentals=0),
    )(head, latents, w_query, w_key, w_value)


def project_kernel(x_ref, wk_ref, wv_ref, k_ref, v_ref):
    n = normed(x_ref[...])
    k_ref[...] = dot(n, wk_ref[...]).astype(BF16)
    v_ref[...] = dot(n, wv_ref[...]).astype(BF16)


def project(prefix, w_key, w_value, tile=512):
    rows, d = prefix.shape
    cols = w_key.shape[1]
    by_row = lambda i: (i, 0)
    whole = lambda i: (0, 0)
    return pl.pallas_call(
        project_kernel,
        grid=(rows // tile,),
        in_specs=[
            pl.BlockSpec((tile, d), by_row),
            pl.BlockSpec((d, cols), whole),
            pl.BlockSpec((d, cols), whole),
        ],
        out_specs=[pl.BlockSpec((tile, cols), by_row)] * 2,
        out_shape=[jax.ShapeDtypeStruct((rows, cols), BF16)] * 2,
        name="project",
        compiler_params=pltpu.CompilerParams(vmem_limit_bytes=50 << 20),
        cost_estimate=pl.CostEstimate(flops=4 * rows * d * cols, bytes_accessed=6 * rows * d, transcendentals=0),
    )(prefix, w_key, w_value)


def attend_kernel(tile, q_ref, k_ref, v_ref, lpos_ref, kpos_ref, o_ref, bias, values):
    latents = bias.shape[0]
    step = pl.program_id(0)

    @pl.when(step == 0)
    def _():
        for t in range(latents // 128):
            at = pl.ds(t * 128, 128)
            own = jnp.transpose(jnp.broadcast_to(lpos_ref[:, at], (128, 128)))
            for c in range(kpos_ref.shape[1] // 128):
                cols = pl.ds(c * 128, 128)
                bias[at, cols] = jnp.where(kpos_ref[:, cols] < own, 0.0, NEG_FILL)

    values[:, :128] = v_ref[...]
    values[:, 128:] = jnp.ones((values.shape[0], 128), BF16)
    lane = iota((1, 128), 1)
    low = lane < HD
    first = step % 2 == 0
    lat_rows = q_ref.shape[2]
    per_tile = tile // lat_rows
    for t in range(latents // tile):
        own = pl.ds(t * per_tile, per_tile)
        q = q_ref[own, 0].reshape(tile, 128)
        sums, stats = [], jnp.zeros((tile, 128), F32)
        for j in range(2):
            qj = jnp.where(low == (j == 0), q, jnp.zeros_like(q))
            s = lax.dot_general(qj, k_ref[...], (((1,), (1,)), ((), ())), preferred_element_type=F32)
            s = s + bias[pl.ds(t * tile, tile), :]
            top = jnp.max(s, axis=1, keepdims=True)
            p = jnp.exp(s - top).astype(BF16)
            total = dot(p, values[...])
            sums.append(total[:, :128])
            t1, rest = split_two(top)
            t2, t3 = split_two(rest)
            s1, s2 = split_two(total[:, 128:])
            piece = jnp.where(
                lane < 4, t1, jnp.where(lane < 8, t2, jnp.where(lane < 12, t3, jnp.where(lane < 16, s1, s2)))
            )
            head = jnp.where(first, j, 2 + j)
            stats = jnp.where((lane % 4 == head) & (lane < 20), piece, stats)
        both = jnp.where(low, sums[0], sums[1]).astype(BF16).reshape(per_tile, lat_rows, 128)
        stats = stats.reshape(per_tile, lat_rows, 128)

        @pl.when(first)
        def _():
            o_ref[own, 0, :, 0:128] = both
            o_ref[own, 0, :, 256:384] = stats.astype(BF16)

        @pl.when(jnp.logical_not(first))
        def _():
            o_ref[own, 0, :, 128:256] = both
            o_ref[own, 0, :, 256:384] = (o_ref[own, 0, :, 256:384].astype(F32) + stats).astype(BF16)


def attend(queries, keys, values, lpos, kpos, tile=128):
    ctx, groups, lat_rows, width = queries.shape
    latents, rows = ctx * lat_rows, keys.shape[0]
    pairs = groups * width // 128
    per = width // 128
    return pl.pallas_call(
        functools.partial(attend_kernel, tile),
        grid=(pairs,),
        in_specs=[
            pl.BlockSpec((ctx, 1, lat_rows, 128), lambda i: (0, i // per, 0, i % per)),
            pl.BlockSpec((rows, 128), lambda i: (0, i)),
            pl.BlockSpec((rows, 128), lambda i: (0, i)),
            pl.BlockSpec((1, latents), lambda i: (0, 0)),
            pl.BlockSpec((1, rows), lambda i: (0, 0)),
        ],
        out_specs=pl.BlockSpec((ctx, 1, lat_rows, width + 128), lambda i: (0, i // per, 0, 0)),
        out_shape=jax.ShapeDtypeStruct((ctx, groups, lat_rows, width + 128), BF16),
        scratch_shapes=[pltpu.VMEM((latents, rows), F32), pltpu.VMEM((rows, 256), BF16)],
        name="attend",
        compiler_params=pltpu.CompilerParams(vmem_limit_bytes=56 << 20),
        cost_estimate=pl.CostEstimate(
            flops=4 * latents * rows * width * groups,
            bytes_accessed=4 * rows * width * groups,
            transcendentals=latents * rows * 2 * pairs,
        ),
    )(queries, keys, values, lpos, kpos)


def combine_kernel(parts_ref, ss_ref, sv_ref, out_ref):
    shards, rows, wide = parts_ref.shape
    parts = parts_ref[...]
    stats = parts[:, :, 256:].reshape(shards * rows, 128)
    r, c = iota((128, 128), 0), iota((128, 128), 1)
    join = ((r < 12) & (r % 4 == c % 4)).astype(BF16)
    tops = dot(stats, join).reshape(shards, rows, 128)
    own = ss_ref[...]
    top = jnp.maximum(jnp.max(tops, axis=0), own)
    scale = jnp.exp(tops - top[None]).reshape(shards * rows, 128)
    high, rest = split_two(scale)
    lane = iota((1, 128), 1)
    pieces = jnp.where(lane < 4, high, jnp.where(lane < 8, rest, 0.0)).astype(BF16)
    r, c = iota((128, wide), 0), iota((128, wide), 1)
    head = jnp.where(c < 256, c // HD, jnp.where((c >= 268) & (c < 276), c % 4, 4))
    spread = ((r < 8) & (r % 4 == head)).astype(BF16)
    scales = dot(pieces, spread).reshape(shards, rows, wide)
    total = jnp.sum(scales * parts.astype(F32), axis=0)
    r, c = iota((128, 256), 0), iota((128, 256), 1)
    denominator = pick_dot(total[:, 256:], ((r >= 12) & (r < 20) & (r % 4 == c // HD)).astype(F32))
    self_weight = pick_dot(jnp.exp(own - top), ((r < 4) & (r == c // HD)).astype(F32))
    numerator = total[:, :256] + self_weight * sv_ref[...].astype(F32)
    out_ref[...] = (numerator / (denominator + self_weight)).astype(BF16)


def combine(parts, self_score, self_value):
    return pl.pallas_call(
        combine_kernel,
        out_shape=jax.ShapeDtypeStruct(self_value.shape, BF16),
        name="combine",
        compiler_params=pltpu.CompilerParams(vmem_limit_bytes=40 << 20),
    )(parts, self_score, self_value)


def per_device(prefix, keep_blocks, keep_count, latent_inputs, latent_pos, w_query, w_key, w_value):
    ctx_size, head_size = lax.axis_size("ctx"), lax.axis_size("head")
    shard = lax.axis_index("ctx") * head_size + lax.axis_index("head")
    rows = prefix.shape[0]
    blocks = rows // BLOCK
    order = jnp.arange(blocks, dtype=jnp.int32)
    match = (keep_blocks.reshape(1, blocks) == order[:, None]) & (order[None, :] < keep_count.reshape(1, 1))
    kept = jnp.repeat(jnp.any(match, axis=1), BLOCK)
    kpos = jnp.where(kept, shard * rows + jnp.arange(rows, dtype=jnp.int32), FAR)[None, :]

    head = lax.axis_index("head").astype(jnp.int32).reshape(1)
    query, self_value, self_score = latent_part(head, latent_inputs, w_query, w_key, w_value)
    lat_rows, width = query.shape
    queries = lax.all_gather(query, AXES, axis=0).reshape(ctx_size, head_size, lat_rows, width)
    keys, values = project(prefix, w_key, w_value)
    parts = attend(queries, keys, values, latent_pos.reshape(1, -1), kpos)
    parts = parts.reshape(ctx_size * head_size, lat_rows, width + 128)
    parts = lax.all_to_all(parts, AXES, 0, 0, tiled=True)
    return combine(parts, self_score, self_value)


def solution(mesh):
    return jax.shard_map(
        per_device,
        mesh=mesh,
        in_specs=(
            P(("ctx", "head"), None),
            P("head", "ctx", None),
            P("head", "ctx"),
            P("ctx", None),
            P(),
            P(None, "head"),
            P(),
            P(),
        ),
        out_specs=P("ctx", "head"),
        check_vma=False,
    )
```

```python
import functools

import jax
import jax.numpy as jnp
from jax import lax
from jax.experimental import pallas as pl
from jax.experimental.pallas import tpu as pltpu
from jax.sharding import PartitionSpec as P

HD = 64
BLOCK = 128
EPSILON = 1e-06
NEG_FILL = -1e30
FAR = 1 << 30
MESH = pl.DeviceIdType.MESH
F32, BF16 = jnp.float32, jnp.bfloat16


def normed(rows):
    wide = rows.astype(F32)
    factor = lax.rsqrt(jnp.mean(wide * wide, axis=-1, keepdims=True) + EPSILON)
    return (wide * factor).astype(BF16)


def dot(a, b):
    return jnp.dot(a, b, preferred_element_type=F32)


def pick_dot(x, ones):
    first = x.astype(BF16)
    rest = x - first.astype(F32)
    second = rest.astype(BF16)
    third = (rest - second.astype(F32)).astype(BF16)
    ones = ones.astype(BF16)
    return dot(first, ones) + dot(second, ones) + dot(third, ones)


def iota(shape, dim):
    return lax.broadcasted_iota(jnp.int32, shape, dim)


def split_two(x):
    high = x.astype(BF16).astype(F32)
    return high, x - high


def combine(parts_ref, own, self_value):
    shards, rows, wide = parts_ref.shape
    parts = parts_ref[...]
    stats = parts[:, :, 256:].reshape(shards * rows, 128)
    r, c = iota((128, 128), 0), iota((128, 128), 1)
    join = ((r < 12) & (r % 4 == c % 4)).astype(BF16)
    tops = dot(stats, join).reshape(shards, rows, 128)
    top = jnp.maximum(jnp.max(tops, axis=0), own)
    scale = jnp.exp(tops - top[None]).reshape(shards * rows, 128)
    high, rest = split_two(scale)
    lane = iota((1, 128), 1)
    pieces = jnp.where(lane < 4, high, jnp.where(lane < 8, rest, 0.0)).astype(BF16)
    r, c = iota((128, wide), 0), iota((128, wide), 1)
    head = jnp.where(c < 256, c // HD, jnp.where((c >= 268) & (c < 276), c % 4, 4))
    spread = ((r < 8) & (r % 4 == head)).astype(BF16)
    scales = dot(pieces, spread).reshape(shards, rows, wide)
    total = jnp.sum(scales * parts.astype(F32), axis=0)
    r, c = iota((128, 256), 0), iota((128, 256), 1)
    denominator = pick_dot(total[:, 256:], ((r >= 12) & (r < 20) & (r % 4 == c // HD)).astype(F32))
    self_weight = pick_dot(jnp.exp(own - top), ((r < 4) & (r == c // HD)).astype(F32))
    numerator = total[:, :256] + self_weight * self_value
    return (numerator / (denominator + self_weight)).astype(BF16)


def totals_of(lane, head, top, weight_sum):
    t1, rest = split_two(top)
    t2, t3 = split_two(rest)
    s1, s2 = split_two(weight_sum)
    piece = jnp.where(lane < 4, t1, jnp.where(lane < 8, t2, jnp.where(lane < 12, t3, jnp.where(lane < 16, s1, s2))))
    return jnp.where((lane % 4 == head) & (lane < 20), piece, 0.0)


def whole_kernel(
    sizes, lat_ref, wq_ref, lpos_ref, kpos_ref, x_hbm, wk_hbm, wv_hbm, out_ref,
    x, wk, wv, keys, values, queries, bias, scores, weights, parts, arrived,
    x_sem, w_sem, q_send, q_recv, p_send, p_recv,
):
    ctx_size, head_size = sizes
    shards = ctx_size * head_size
    me_c, me_h = lax.axis_index("ctx"), lax.axis_index("head")
    me = me_c * head_size + me_h
    rows = x.shape[0]
    tile = 512
    copies = [pltpu.make_async_copy(wk_hbm, wk, w_sem.at[0]), pltpu.make_async_copy(wv_hbm, wv, w_sem.at[1])]
    copies[0].start()

    def x_copy(t):
        at = pl.ds(pl.multiple_of(t * tile, tile), tile)
        return pltpu.make_async_copy(x_hbm.at[at], x.at[at], x_sem.at[t])

    x_copy(0).start()
    copies[1].start()
    for t in range(1, rows // tile):
        x_copy(t).start()

    barrier = pltpu.get_barrier_semaphore()

    def peer(i):
        other = lax.rem(me + i, shards)
        return (lax.div(other, head_size), lax.rem(other, head_size))

    def greet(i, carry):
        pl.semaphore_signal(barrier, inc=1, device_id=peer(i), device_id_type=MESH)
        return carry

    lax.fori_loop(1, shards, greet, 0)

    lat_n = normed(lat_ref[...])
    query = (dot(lat_n, wq_ref[...]) * HD ** (-0.5)).astype(BF16)
    queries[me_h * ctx_size + me_c] = query
    pl.semaphore_wait(barrier, shards - 1)

    def send_query(i, carry):
        mine = queries.at[me_h * ctx_size + me_c]
        pltpu.make_async_remote_copy(
            src_ref=mine, dst_ref=mine, send_sem=q_send, recv_sem=q_recv, device_id=peer(i), device_id_type=MESH
        ).start()
        return carry

    lax.fori_loop(1, shards, send_query, 0)

    lane = iota((1, 128), 1)
    low = lane < HD
    latents, lat_rows = bias.shape[0], lat_ref.shape[0]
    for t in range(latents // 128):
        at = pl.ds(t * 128, 128)
        own = jnp.transpose(jnp.broadcast_to(lpos_ref[:, at], (128, 128)))
        for c in range(rows // 128):
            cols = pl.ds(c * 128, 128)
            bias[at, cols] = jnp.where(kpos_ref[:, cols] < own, 0.0, NEG_FILL)
    values[:, :, 128:] = jnp.ones(values.shape[:2] + (128,), BF16)

    copies[0].wait()
    copies[1].wait()
    pairs = keys.shape[0]

    def project(t, carry):
        x_copy(t).wait()
        at = pl.ds(pl.multiple_of(t * tile, tile), tile)
        n = normed(x[at, :])
        k = dot(n, wk[...]).astype(BF16)
        for p in range(pairs):
            keys[p, at, :] = k[:, p * 128:(p + 1) * 128]
        v = dot(n, wv[...]).astype(BF16)
        for p in range(pairs):
            values[p, at, 0:128] = v[:, p * 128:(p + 1) * 128]
        return carry

    lax.fori_loop(0, rows // tile, project, 0)

    width = wq_ref.shape[1]
    mine = pl.ds(pl.multiple_of(me_h * width, width), width)
    self_key = dot(lat_n, wk[:, mine]).astype(BF16)
    self_value = dot(lat_n, wv[:, mine]).astype(BF16).astype(F32)
    prod = query.astype(F32) * self_key.astype(F32)
    self_score = pick_dot(prod, iota((width, 128), 0) // HD == iota((width, 128), 1) % (width // HD))

    count = pl.ds(0, shards - 1)
    landed = queries.at[count]
    pltpu.make_async_copy(landed, landed, q_recv).wait()
    pltpu.make_async_copy(landed, landed, q_send).wait()

    step_rows = 128
    per = step_rows // lat_rows
    units = [(t, j) for t in range(latents // step_rows) for j in range(2)]
    chunk, part_rows = 256, 1024

    def group(step, carry):
        g = lax.rem(me_h + 1 + step, head_size)
        top = None
        stats = None
        for u in range(-1, len(units)):
            q = peak = total = None
            nxt = u + 1
            if nxt < len(units):
                t, j = units[nxt]
                q = queries[pl.ds(g * ctx_size + t * per, per), :, j * 128:(j + 1) * 128].reshape(step_rows, 128)
                zero = jnp.zeros_like(q)
                q = jnp.concatenate([jnp.where(low, q, zero), jnp.where(low, zero, q)], 0)
            for c in range(rows // chunk):
                at = pl.ds(c * chunk, chunk)
                if nxt < len(units):
                    t, j = units[nxt]
                    s = lax.dot_general(
                        q, keys[g * 2 + j, at, :], (((1,), (1,)), ((), ())), preferred_element_type=F32
                    )
                    off = bias[pl.ds(t * step_rows, step_rows), at]
                    s = jnp.concatenate([s[:step_rows] + off, s[step_rows:] + off], 0)
                    scores[nxt % 2, :, at] = s
                    for i in range(chunk // 128):
                        piece = s[:, i * 128:(i + 1) * 128]
                        peak = piece if peak is None else jnp.maximum(peak, piece)
                if u >= 0:
                    t, j = units[u]
                    weights[:, at] = jnp.exp(scores[u % 2, :, at] - top).astype(BF16)
                    if (c + 1) * chunk % part_rows == 0:
                        at = pl.ds((c + 1) * chunk - part_rows, part_rows)
                        more = dot(weights[:, at], values[g * 2 + j, at, :])
                        total = more if total is None else total + more
            if u >= 0:
                t, j = units[u]
                own = pl.ds(t * per, per)
                both = jnp.where(low, total[:step_rows, :128], total[step_rows:, :128]).astype(BF16)
                parts[g, own, :, j * 128:(j + 1) * 128] = both.reshape(per, lat_rows, 128)
                new = totals_of(lane, 2 * j, top[:step_rows], total[:step_rows, 128:])
                new = new + totals_of(lane, 2 * j + 1, top[step_rows:], total[step_rows:, 128:])
                if j == 0:
                    stats = new
                else:
                    parts[g, own, :, 256:384] = (stats + new).astype(BF16).reshape(per, lat_rows, 128)
            if peak is not None:
                top = jnp.max(peak, axis=1, keepdims=True)

        def send_part(i, carry):
            c = lax.rem(me_c + i, ctx_size)
            pltpu.make_async_remote_copy(
                src_ref=parts.at[g, c], dst_ref=arrived.at[me], send_sem=p_send, recv_sem=p_recv,
                device_id=(c, g), device_id_type=MESH,
            ).start()
            return carry

        lax.fori_loop(lax.div(step + 1, head_size), ctx_size, send_part, 0)
        return carry

    lax.fori_loop(0, head_size, group, 0)
    arrived[me] = parts[me_h, me_c]
    landed = arrived.at[count]
    pltpu.make_async_copy(landed, landed, p_recv).wait()
    out_ref[...] = combine(arrived, self_score, self_value)
    pltpu.make_async_copy(landed, landed, p_send).wait()


def per_device(prefix, keep_blocks, keep_count, latent_inputs, latent_pos, w_query, w_key, w_value):
    ctx_size, head_size = lax.axis_size("ctx"), lax.axis_size("head")
    shard = lax.axis_index("ctx") * head_size + lax.axis_index("head")
    rows, d = prefix.shape
    blocks = rows // BLOCK
    order = jnp.arange(blocks, dtype=jnp.int32)
    match = (keep_blocks.reshape(1, blocks) == order[:, None]) & (order[None, :] < keep_count.reshape(1, 1))
    kept = jnp.repeat(jnp.any(match, axis=1), BLOCK)
    kpos = jnp.where(kept, shard * rows + jnp.arange(rows, dtype=jnp.int32), FAR)[None, :]
    lat_rows, width = latent_inputs.shape[0], w_query.shape[1]
    latents, cols = lat_rows * ctx_size, width * head_size
    pairs = cols // 128
    vmem = pl.BlockSpec(memory_space=pltpu.VMEM)
    hbm = pl.BlockSpec(memory_space=pl.ANY)
    dma = pltpu.SemaphoreType.DMA
    return pl.pallas_call(
        functools.partial(whole_kernel, (ctx_size, head_size)),
        in_specs=[vmem] * 4 + [hbm] * 3,
        out_specs=vmem,
        out_shape=jax.ShapeDtypeStruct((lat_rows, width), BF16),
        scratch_shapes=[
            pltpu.VMEM((rows, d), BF16),
            pltpu.VMEM((d, cols), BF16),
            pltpu.VMEM((d, cols), BF16),
            pltpu.VMEM((pairs, rows, 128), BF16),
            pltpu.VMEM((pairs, rows, 256), BF16),
            pltpu.VMEM((head_size * ctx_size, lat_rows, width), BF16),
            pltpu.VMEM((latents, rows), F32),
            pltpu.VMEM((2, 256, rows), F32),
            pltpu.VMEM((256, rows), BF16),
            pltpu.VMEM((head_size, ctx_size, lat_rows, width + 128), BF16),
            pltpu.VMEM((ctx_size * head_size, lat_rows, width + 128), BF16),
            dma((rows // 512,)),
            dma((2,)),
            dma,
            dma,
            dma,
            dma,
        ],
        name="whole",
        compiler_params=pltpu.CompilerParams(
            collective_id=0, has_side_effects=True, vmem_limit_bytes=60 << 20
        ),
        cost_estimate=pl.CostEstimate(
            flops=4 * rows * d * cols + 4 * latents * rows * cols,
            bytes_accessed=2 * rows * d + 4 * d * cols,
            transcendentals=latents * rows * 2 * pairs,
        ),
    )(latent_inputs, w_query, latent_pos.reshape(1, -1), kpos, prefix, w_key, w_value)


def solution(mesh):
    return jax.shard_map(
        per_device,
        mesh=mesh,
        in_specs=(
            P(("ctx", "head"), None),
            P("head", "ctx", None),
            P("head", "ctx"),
            P("ctx", None),
            P(),
            P(None, "head"),
            P(),
            P(),
        ),
        out_specs=P("ctx", "head"),
        check_vma=False,
    )
```

```python
import functools

import jax
import jax.numpy as jnp
from jax import lax
from jax.experimental import pallas as pl
from jax.experimental.pallas import tpu as pltpu
from jax.sharding import PartitionSpec as P

HD = 64
BLOCK = 128
EPSILON = 1e-06
NEG_FILL = -1e30
FAR = 1 << 30
MESH = pl.DeviceIdType.MESH
F32, BF16 = jnp.float32, jnp.bfloat16


def normed(rows):
    wide = rows.astype(F32)
    factor = lax.rsqrt(jnp.mean(wide * wide, axis=-1, keepdims=True) + EPSILON)
    return (wide * factor).astype(BF16)


def dot(a, b):
    return jnp.dot(a, b, preferred_element_type=F32)


def pick_dot(x, ones):
    first = x.astype(BF16)
    rest = x - first.astype(F32)
    second = rest.astype(BF16)
    third = (rest - second.astype(F32)).astype(BF16)
    ones = ones.astype(BF16)
    return dot(first, ones) + dot(second, ones) + dot(third, ones)


def iota(shape, dim):
    return lax.broadcasted_iota(jnp.int32, shape, dim)


def split_two(x):
    high = x.astype(BF16).astype(F32)
    return high, x - high


def spread_scale(scale, wide):
    high, rest = split_two(scale)
    lane = iota((1, 128), 1)
    pieces = jnp.where(lane < 4, high, jnp.where(lane < 8, rest, 0.0)).astype(BF16)
    r, c = iota((128, wide), 0), iota((128, wide), 1)
    head = jnp.where(c < 256, c // HD, jnp.where((c >= 268) & (c < 276), c % 4, 4))
    return dot(pieces, ((r < 8) & (r % 4 == head)).astype(BF16))


def combine(parts_ref, own, self_value):
    shards, rows, wide = parts_ref.shape
    parts = parts_ref[...]
    stats = parts[:, :, 256:].reshape(shards * rows, 128)
    r, c = iota((128, 128), 0), iota((128, 128), 1)
    join = ((r < 12) & (r % 4 == c % 4)).astype(BF16)
    tops = dot(stats, join).reshape(shards, rows, 128)
    top = jnp.maximum(jnp.max(tops, axis=0), own)
    scale = jnp.exp(tops - top[None]).reshape(shards * rows, 128)
    scales = spread_scale(scale, wide).reshape(shards, rows, wide)
    total = jnp.sum(scales * parts.astype(F32), axis=0)
    r, c = iota((128, 256), 0), iota((128, 256), 1)
    denominator = pick_dot(total[:, 256:], ((r >= 12) & (r < 20) & (r % 4 == c // HD)).astype(F32))
    self_weight = pick_dot(jnp.exp(own - top), ((r < 4) & (r == c // HD)).astype(F32))
    numerator = total[:, :256] + self_weight * self_value
    return (numerator / (denominator + self_weight)).astype(BF16)


def pieces_of(lane, top, weight_sum):
    t1, rest = split_two(top)
    t2, t3 = split_two(rest)
    s1, s2 = split_two(weight_sum)
    piece = jnp.where(lane < 4, t1, jnp.where(lane < 8, t2, jnp.where(lane < 12, t3, jnp.where(lane < 16, s1, s2))))
    return jnp.where(lane < 20, piece, 0.0)


def totals_of(lane, head, top, weight_sum):
    return jnp.where(lane % 4 == head, pieces_of(lane, top, weight_sum), 0.0)


def merge(mine, theirs):
    rows, wide = mine.shape
    both = jnp.concatenate([mine, theirs], 0)
    r, c = iota((128, 128), 0), iota((128, 128), 1)
    tops = dot(both[:, 256:], ((r < 12) & (r % 4 == c % 4)).astype(BF16))
    top = jnp.maximum(tops[:rows], tops[rows:])
    scaled = both.astype(F32) * spread_scale(jnp.exp(tops - jnp.concatenate([top, top], 0)), wide)
    total = scaled[:rows] + scaled[rows:]
    weight_sum = pick_dot(total[:, 256:], (r >= 12) & (r < 20) & (r % 4 == c % 4))
    return total[:, :256], pieces_of(iota((1, 128), 1), top, weight_sum)


def whole_kernel(
    sizes, lat_ref, wq_ref, lpos_ref, kb_ref, kc_ref, x_hbm, wk_hbm, wv_hbm, out_ref,
    x, wk, wv, keys, values, own_query, queries, bias, scores, weights, tops, own, other, merged, arrived,
    x_sem, w_sem, q_send, q_recv, f_send, f_recv, o_send, o_recv, p_send, p_recv,
):
    ctx_size, planes = sizes
    chips = ctx_size // 2
    near = chips // 2
    me_c, me_h = lax.axis_index("ctx"), lax.axis_index("head")
    me_p, me_k = lax.div(me_c, 2), lax.rem(me_c, 2)
    me_half = lax.div(me_p, near)
    sibling = (me_p * 2 + 1 - me_k, me_h)
    rows = x.shape[0]
    tile = 512

    def x_copy(t):
        at = pl.ds(pl.multiple_of(t * tile, tile), tile)
        return pltpu.make_async_copy(x_hbm.at[at], x.at[at], x_sem.at[t])

    wk_copy = pltpu.make_async_copy(wk_hbm, wk, w_sem.at[0])
    wv_copy = pltpu.make_async_copy(wv_hbm, wv, w_sem.at[1])
    wk_copy.start()
    x_copy(0).start()
    wv_copy.start()
    for t in range(1, rows // tile):
        x_copy(t).start()

    barrier = pltpu.get_barrier_semaphore()

    def peer(i):
        away = 1 + lax.div(i, chips)
        plane = lax.rem(jnp.where(me_half == 0, me_h + planes - away, me_h + away), planes)
        chip = lax.rem(me_p + lax.rem(i, chips), chips)
        return (chip * 2 + me_k, plane)

    def greet(i, carry):
        pl.semaphore_signal(barrier, inc=1, device_id=peer(i), device_id_type=MESH)
        return carry

    own_place = chips * (planes - 1)
    lax.fori_loop(0, own_place, greet, 0)
    lax.fori_loop(own_place + 1, chips * planes, greet, 0)
    pl.semaphore_signal(barrier, inc=1, device_id=sibling, device_id_type=MESH)

    lat_n = normed(lat_ref[...])
    query = (dot(lat_n, wq_ref[...]) * HD ** (-0.5)).astype(BF16)
    own_query[...] = query
    lat_rows = lat_ref.shape[0]
    lane = iota((1, 128), 1)
    low = lane < HD

    first_pos = (me_c * planes + me_h) * rows
    for half in range(2):
        span = near * 2 * lat_rows
        at = pl.ds(half * span, span)
        pos = jnp.transpose(jnp.broadcast_to(lpos_ref[:, at], (128, span))).reshape(near, 2, lat_rows, 128)
        for k in range(2):
            pos_k = pos[:, k].reshape(near * lat_rows, 128)
            for b in range(rows // BLOCK):
                hit = (kb_ref[...] == b) & (iota(kb_ref.shape, 1) < kc_ref[...])
                kept = jnp.max(jnp.where(hit, 1.0, 0.0), axis=1, keepdims=True)
                at_b = pl.ds(b * BLOCK, BLOCK)
                key_pos = jnp.where(kept > 0.5, first_pos + b * BLOCK + lane, FAR)
                bias[half * 2 + k, :, at_b] = jnp.where(key_pos < pos_k, 0.0, NEG_FILL)
    values[:, :, 128:] = jnp.ones(values.shape[:2] + (128,), BF16)

    pl.semaphore_wait(barrier, chips * planes)

    def q_slot(g, half, k):
        return pl.multiple_of(((g * 2 + half) * 2 + k) * near, near)

    own_slot = queries.at[q_slot(me_h, me_half, me_k) + lax.rem(me_p, near)]
    own_sem = q_recv.at[me_h * 2 + me_half]

    def send_query(i, carry):
        pltpu.make_async_remote_copy(
            src_ref=own_query, dst_ref=own_slot, send_sem=q_send, recv_sem=own_sem,
            device_id=peer(i), device_id_type=MESH,
        ).start()
        return carry

    lax.fori_loop(0, own_place, send_query, 0)
    pltpu.make_async_copy(own_query, own_slot, own_sem).start()
    lax.fori_loop(own_place + 1, chips * planes, send_query, 0)

    wk_copy.wait()
    wv_copy.wait()
    pairs = keys.shape[0]

    def project(t, carry):
        x_copy(t).wait()
        at = pl.ds(pl.multiple_of(t * tile, tile), tile)
        n = normed(x[at, :])
        k = dot(n, wk[...]).astype(BF16)
        for p in range(pairs):
            keys[p, at, :] = k[:, p * 128:(p + 1) * 128]
        v = dot(n, wv[...]).astype(BF16)
        for p in range(pairs):
            values[p, at, 0:128] = v[:, p * 128:(p + 1) * 128]
        return carry

    def groups(step):
        return lax.rem(me_h + 1 + step, planes), lax.rem(me_h + 2 * planes - 1 - step, planes)

    def forward(step):
        for half, g in enumerate(groups(step)):
            slots = queries.at[pl.ds(q_slot(g, half, me_k), near)]
            pltpu.make_async_copy(slots, slots, q_recv.at[g * 2 + half]).wait()
            pltpu.make_async_remote_copy(
                src_ref=slots, dst_ref=slots, send_sem=f_send, recv_sem=f_recv.at[g * 2 + half],
                device_id=sibling, device_id_type=MESH,
            ).start()

    def forwarded(step):
        for half, g in enumerate(groups(step)):
            slots = queries.at[pl.ds(q_slot(g, half, 1 - me_k), near)]
            pltpu.make_async_copy(slots, slots, f_recv.at[g * 2 + half]).wait()

    lax.fori_loop(0, rows // tile, project, 0)
    forward(0)
    forwarded(0)

    step_rows = near * lat_rows
    units = [(half, j) for half in range(2) for j in range(2)]
    chunk, part_rows = 256, 1024
    last = 2 * planes - 1

    def where_at(it):
        return lax.div(it, 2), lax.rem(me_k + 1 + it, 2)

    def load_query(it, unit):
        half, j = unit
        step, k = where_at(it)
        g = groups(step)[half]
        q = queries[pl.ds(q_slot(g, half, k), near), :, j * 128:(j + 1) * 128].reshape(step_rows, 128)
        zero = jnp.zeros_like(q)
        return jnp.concatenate([jnp.where(low, q, zero), jnp.where(low, zero, q)], 0), g * 2 + j, half * 2 + k

    def score(u, q, pair, tile_at, at, peak):
        s = lax.dot_general(q, keys[pair, at, :], (((1,), (1,)), ((), ())), preferred_element_type=F32)
        off = bias[tile_at, :, at]
        s = jnp.concatenate([s[:step_rows] + off, s[step_rows:] + off], 0)
        scores[u % 2, :, at] = s
        for i in range(chunk // 128):
            piece = s[:, i * 128:(i + 1) * 128]
            peak = piece if peak is None else jnp.maximum(peak, piece)
        return peak

    def top_of(peak):
        return jnp.broadcast_to(jnp.max(peak, axis=1, keepdims=True), peak.shape)

    peak = None
    loaded = load_query(0, units[0])
    for c in range(rows // chunk):
        peak = score(0, *loaded, pl.ds(c * chunk, chunk), peak)
    tops[...] = top_of(peak)

    def iteration(it, carry):
        step, _ = where_at(it)
        odd = lax.rem(it, 2)
        more = step < planes - 1

        @pl.when((odd == 0) & more)
        def _():
            forward(step + 1)

        @pl.when((odd == 1) & more)
        def _():
            forwarded(step + 1)

        here = groups(step)
        top = tops[...]
        stats = None
        for u in range(len(units)):
            nxt = u + 1
            if nxt < len(units):
                loaded = load_query(it, units[nxt])
            else:
                loaded = load_query(jnp.minimum(it + 1, last), units[0])
            half, j = units[u]
            peak = total = None
            for c in range(rows // chunk):
                at = pl.ds(c * chunk, chunk)
                peak = score(nxt, *loaded, at, peak)
                wide_top = jnp.concatenate([top] * (chunk // 128), 1)
                weights[:, at] = jnp.exp(scores[u % 2, :, at] - wide_top).astype(BF16)
                if (c + 1) * chunk % part_rows == 0:
                    at = pl.ds((c + 1) * chunk - part_rows, part_rows)
                    part = dot(weights[:, at], values[here[half] * 2 + j, at, :])
                    total = part if total is None else total + part
            both = jnp.where(low, total[:step_rows, :128], total[step_rows:, :128]).astype(BF16)
            own[it, half, :, :, j * 128:(j + 1) * 128] = both.reshape(near, lat_rows, 128)
            new = totals_of(lane, 2 * j, top[:step_rows], total[:step_rows, 128:])
            new = new + totals_of(lane, 2 * j + 1, top[step_rows:], total[step_rows:, 128:])
            if j == 0:
                stats = new
            else:
                own[it, half, :, :, 256:384] = (stats + new).astype(BF16).reshape(near, lat_rows, 128)
            top = top_of(peak)
        tops[...] = top

        @pl.when(odd == 0)
        def _():
            pltpu.make_async_remote_copy(
                src_ref=own.at[it], dst_ref=other.at[step], send_sem=o_send, recv_sem=o_recv.at[step],
                device_id=sibling, device_id_type=MESH,
            ).start()

        @pl.when(odd == 1)
        def _():
            pltpu.make_async_copy(other.at[step], other.at[step], o_recv.at[step]).wait()
            shape = own.shape[1:]
            flat = (shape[0] * shape[1] * shape[2], shape[3])
            weighted, stats = merge(own[it].reshape(flat), other[step].reshape(flat))
            merged[step, :, :, :, 0:256] = weighted.astype(BF16).reshape(shape[:3] + (256,))
            merged[step, :, :, :, 256:384] = stats.astype(BF16).reshape(shape[:3] + (128,))

            def send_part(i, carry):
                chip = lax.rem(me_p + i, chips)
                half = lax.div(chip, near)
                g = jnp.where(half == 0, here[0], here[1])
                pltpu.make_async_remote_copy(
                    src_ref=merged.at[step, half, lax.rem(chip, near)], dst_ref=arrived.at[me_h * chips + me_p],
                    send_sem=p_send, recv_sem=p_recv, device_id=(chip * 2 + me_k, g), device_id_type=MESH,
                ).start()
                return carry

            lax.fori_loop(lax.div(step + 1, planes), chips, send_part, 0)

        return carry

    lax.fori_loop(0, last + 1, iteration, 0)
    pltpu.make_async_copy(
        merged.at[planes - 1, me_half, lax.rem(me_p, near)], arrived.at[me_h * chips + me_p], p_recv
    ).start()

    width = wq_ref.shape[1]
    mine = pl.ds(pl.multiple_of(me_h * width, width), width)
    self_key = dot(lat_n, wk[:, mine]).astype(BF16)
    self_value = dot(lat_n, wv[:, mine]).astype(BF16).astype(F32)
    prod = query.astype(F32) * self_key.astype(F32)
    self_score = pick_dot(prod, iota((width, 128), 0) // HD == iota((width, 128), 1) % (width // HD))

    pltpu.make_async_copy(arrived, arrived, p_recv).wait()
    out_ref[...] = combine(arrived, self_score, self_value)
    sent = queries.at[pl.ds(0, chips * planes - 1)]
    pltpu.make_async_copy(sent, sent, q_send).wait()
    sent = queries.at[pl.ds(0, chips * planes)]
    pltpu.make_async_copy(sent, sent, f_send).wait()
    pltpu.make_async_copy(other, other, o_send).wait()
    sent = arrived.at[pl.ds(0, chips * planes - 1)]
    pltpu.make_async_copy(sent, sent, p_send).wait()


def per_device(prefix, keep_blocks, keep_count, latent_inputs, latent_pos, w_query, w_key, w_value):
    ctx_size, head_size = lax.axis_size("ctx"), lax.axis_size("head")
    rows, d = prefix.shape
    lat_rows, width = latent_inputs.shape[0], w_query.shape[1]
    latents, cols = lat_rows * ctx_size, width * head_size
    pairs = cols // 128
    shards = ctx_size * head_size
    near = ctx_size // 4
    wide = width + 128
    vmem = pl.BlockSpec(memory_space=pltpu.VMEM)
    hbm = pl.BlockSpec(memory_space=pl.ANY)
    dma = pltpu.SemaphoreType.DMA
    return pl.pallas_call(
        functools.partial(whole_kernel, (ctx_size, head_size)),
        in_specs=[vmem] * 5 + [hbm] * 3,
        out_specs=vmem,
        out_shape=jax.ShapeDtypeStruct((lat_rows, width), BF16),
        scratch_shapes=[
            pltpu.VMEM((rows, d), BF16),
            pltpu.VMEM((d, cols), BF16),
            pltpu.VMEM((d, cols), BF16),
            pltpu.VMEM((pairs, rows, 128), BF16),
            pltpu.VMEM((pairs, rows, 256), BF16),
            pltpu.VMEM((lat_rows, width), BF16),
            pltpu.VMEM((shards, lat_rows, width), BF16),
            pltpu.VMEM((4, latents // 4, rows), F32),
            pltpu.VMEM((2, 256, rows), F32),
            pltpu.VMEM((256, rows), BF16),
            pltpu.VMEM((256, 128), F32),
            pltpu.VMEM((2 * head_size, 2, near, lat_rows, wide), BF16),
            pltpu.VMEM((head_size, 2, near, lat_rows, wide), BF16),
            pltpu.VMEM((head_size, 2, near, lat_rows, wide), BF16),
            pltpu.VMEM((shards // 2, lat_rows, wide), BF16),
            dma((rows // 512,)),
            dma((2,)),
            dma,
            dma((2 * head_size,)),
            dma,
            dma((2 * head_size,)),
            dma,
            dma((head_size,)),
            dma,
            dma,
        ],
        name="whole",
        compiler_params=pltpu.CompilerParams(
            collective_id=0, has_side_effects=True, vmem_limit_bytes=60 << 20
        ),
        cost_estimate=pl.CostEstimate(
            flops=4 * rows * d * cols + 4 * latents * rows * cols,
            bytes_accessed=2 * rows * d + 4 * d * cols,
            transcendentals=latents * rows * 2 * pairs,
        ),
    )(
        latent_inputs, w_query, latent_pos.reshape(1, latents),
        keep_blocks.reshape(1, -1), keep_count.reshape(1, 1), prefix, w_key, w_value,
    )


def solution(mesh):
    return jax.shard_map(
        per_device,
        mesh=mesh,
        in_specs=(
            P(("ctx", "head"), None),
            P("head", "ctx", None),
            P("head", "ctx"),
            P("ctx", None),
            P(),
            P(None, "head"),
            P(),
            P(),
        ),
        out_specs=P("ctx", "head"),
        check_vma=False,
    )
```

```python
import functools

import jax
import jax.numpy as jnp
from jax import lax
from jax.experimental import pallas as pl
from jax.experimental.pallas import tpu as pltpu
from jax.sharding import PartitionSpec as P

HD = 64
BLOCK = 128
EPSILON = 1e-06
NEG_FILL = -1e30
FAR = 1 << 30
MESH = pl.DeviceIdType.MESH
F32, BF16 = jnp.float32, jnp.bfloat16


def normed(rows):
    wide = rows.astype(F32)
    factor = lax.rsqrt(jnp.mean(wide * wide, axis=-1, keepdims=True) + EPSILON)
    return (wide * factor).astype(BF16)


def dot(a, b):
    return jnp.dot(a, b, preferred_element_type=F32)


def pick_dot(x, ones):
    first = x.astype(BF16)
    rest = x - first.astype(F32)
    second = rest.astype(BF16)
    third = (rest - second.astype(F32)).astype(BF16)
    ones = ones.astype(BF16)
    return dot(first, ones) + dot(second, ones) + dot(third, ones)


def iota(shape, dim):
    return lax.broadcasted_iota(jnp.int32, shape, dim)


def split_two(x):
    high = x.astype(BF16).astype(F32)
    return high, x - high


def spread_scale(scale, wide):
    high, rest = split_two(scale)
    lane = iota((1, 128), 1)
    pieces = jnp.where(lane < 4, high, jnp.where(lane < 8, rest, 0.0)).astype(BF16)
    r, c = iota((128, wide), 0), iota((128, wide), 1)
    head = jnp.where(c < 256, c // HD, jnp.where((c >= 268) & (c < 276), c % 4, 4))
    return dot(pieces, ((r < 8) & (r % 4 == head)).astype(BF16))


def combine(parts_ref, own, self_value):
    shards, rows, wide = parts_ref.shape
    parts = parts_ref[...]
    stats = parts[:, :, 256:].reshape(shards * rows, 128)
    r, c = iota((128, 128), 0), iota((128, 128), 1)
    join = ((r < 12) & (r % 4 == c % 4)).astype(BF16)
    tops = dot(stats, join).reshape(shards, rows, 128)
    top = jnp.maximum(jnp.max(tops, axis=0), own)
    scale = jnp.exp(tops - top[None]).reshape(shards * rows, 128)
    scales = spread_scale(scale, wide).reshape(shards, rows, wide)
    total = jnp.sum(scales * parts.astype(F32), axis=0)
    r, c = iota((128, 256), 0), iota((128, 256), 1)
    denominator = pick_dot(total[:, 256:], ((r >= 12) & (r < 20) & (r % 4 == c // HD)).astype(F32))
    self_weight = pick_dot(jnp.exp(own - top), ((r < 4) & (r == c // HD)).astype(F32))
    numerator = total[:, :256] + self_weight * self_value
    return (numerator / (denominator + self_weight)).astype(BF16)


def pieces_of(lane, top, weight_sum):
    t1, rest = split_two(top)
    t2, t3 = split_two(rest)
    s1, s2 = split_two(weight_sum)
    piece = jnp.where(lane < 4, t1, jnp.where(lane < 8, t2, jnp.where(lane < 12, t3, jnp.where(lane < 16, s1, s2))))
    return jnp.where(lane < 20, piece, 0.0)


def totals_of(lane, head, top, weight_sum):
    return jnp.where(lane % 4 == head, pieces_of(lane, top, weight_sum), 0.0)


def merge(blocks):
    rows, wide = blocks[0].shape
    many = jnp.concatenate(blocks, 0)
    r, c = iota((128, 128), 0), iota((128, 128), 1)
    tops = dot(many[:, 256:], ((r < 12) & (r % 4 == c % 4)).astype(BF16))
    cut = lambda whole: [whole[i * rows:(i + 1) * rows] for i in range(len(blocks))]
    top = functools.reduce(jnp.maximum, cut(tops))
    scale = jnp.exp(tops - jnp.concatenate([top] * len(blocks), 0))
    total = sum(cut(many.astype(F32) * spread_scale(scale, wide)))
    weight_sum = pick_dot(total[:, 256:], (r >= 12) & (r < 20) & (r % 4 == c % 4))
    stats = pieces_of(iota((1, 128), 1), top, weight_sum)
    return jnp.concatenate([total[:, :256], stats], 1).astype(BF16)


def whole_kernel(
    sizes, lat_ref, wq_ref, lpos_ref, kb_ref, kc_ref, x_hbm, wk_hbm, wv_hbm, out_ref,
    x, wk, wv, keys, values, queries, plane_query, bias, scores, weights, tops, own, other, merged, along_z, arrived,
    x_sem, w_sem, s_send, s_recv, q_send, q_recv, f_send, f_recv, o_send, o_recv, z_send, z_recv, p_send, p_recv,
):
    ctx_size, planes = sizes
    chips = ctx_size // 2
    near = chips // 2
    me_c, me_h = lax.axis_index("ctx"), lax.axis_index("head")
    me_p, me_k = lax.div(me_c, 2), lax.rem(me_c, 2)
    me_half = lax.div(me_p, near)
    sibling = (me_p * 2 + 1 - me_k, me_h)
    rows = x.shape[0]
    tile = 512

    def x_copy(t):
        at = pl.ds(pl.multiple_of(t * tile, tile), tile)
        return pltpu.make_async_copy(x_hbm.at[at], x.at[at], x_sem.at[t])

    wk_copy = pltpu.make_async_copy(wk_hbm, wk, w_sem.at[0])
    wv_copy = pltpu.make_async_copy(wv_hbm, wv, w_sem.at[1])
    wk_copy.start()
    x_copy(0).start()
    wv_copy.start()
    for t in range(1, rows // tile):
        x_copy(t).start()

    barrier = pltpu.get_barrier_semaphore()

    def in_plane(away):
        return (me_c, lax.rem(me_h + away, planes))

    def in_chip(away):
        return (lax.rem(me_p + away, chips) * 2 + me_k, me_h)

    def greet(device):
        pl.semaphore_signal(barrier, inc=1, device_id=device, device_id_type=MESH)

    for away in range(1, planes):
        greet(in_plane(away))
    greet(sibling)

    def greet_chip(away, carry):
        greet(in_chip(away))
        return carry

    lax.fori_loop(1, chips, greet_chip, 0)

    lat_n = normed(lat_ref[...])
    query = (dot(lat_n, wq_ref[...]) * HD ** (-0.5)).astype(BF16)
    plane_query[me_h] = query
    lat_rows = lat_ref.shape[0]
    lane = iota((1, 128), 1)
    low = lane < HD

    first_pos = (me_c * planes + me_h) * rows
    for half in range(2):
        span = near * 2 * lat_rows
        at = pl.ds(half * span, span)
        pos = jnp.transpose(jnp.broadcast_to(lpos_ref[:, at], (128, span))).reshape(near, 2, lat_rows, 128)
        for k in range(2):
            pos_k = pos[:, k].reshape(near * lat_rows, 128)
            for b in range(rows // BLOCK):
                hit = (kb_ref[...] == b) & (iota(kb_ref.shape, 1) < kc_ref[...])
                kept = jnp.max(jnp.where(hit, 1.0, 0.0), axis=1, keepdims=True)
                at_b = pl.ds(b * BLOCK, BLOCK)
                key_pos = jnp.where(kept > 0.5, first_pos + b * BLOCK + lane, FAR)
                bias[half * 2 + k, :, at_b] = jnp.where(key_pos < pos_k, 0.0, NEG_FILL)
    values[:, :, 128:] = jnp.ones(values.shape[:2] + (128,), BF16)

    wk_copy.wait()
    wv_copy.wait()
    pairs = keys.shape[0]

    def project(t, carry):
        x_copy(t).wait()
        at = pl.ds(pl.multiple_of(t * tile, tile), tile)
        n = normed(x[at, :])
        k = dot(n, wk[...]).astype(BF16)
        for p in range(pairs):
            keys[p, at, :] = k[:, p * 128:(p + 1) * 128]
        v = dot(n, wv[...]).astype(BF16)
        for p in range(pairs):
            values[p, at, 0:128] = v[:, p * 128:(p + 1) * 128]
        return carry

    def groups(step):
        return lax.rem(me_h + 1 + step, planes), lax.rem(me_h + 2 * planes - 1 - step, planes)

    def send_along_z():
        for away in range(1, planes):
            mine = plane_query.at[me_h]
            pltpu.make_async_remote_copy(
                src_ref=mine, dst_ref=mine, send_sem=s_send, recv_sem=s_recv,
                device_id=in_plane(away), device_id_type=MESH,
            ).start()

    def send_in_plane():
        some = plane_query.at[pl.ds(0, planes - 1)]
        pltpu.make_async_copy(some, some, s_recv).wait()
        slots = queries.at[:, me_half, me_k, lax.rem(me_p, near)]

        def send(away, carry):
            pltpu.make_async_remote_copy(
                src_ref=plane_query, dst_ref=slots, send_sem=q_send, recv_sem=q_recv,
                device_id=in_chip(away), device_id_type=MESH,
            ).start()
            return carry

        lax.fori_loop(1, chips, send, 0)
        pltpu.make_async_copy(plane_query, slots, q_recv).start()

    def forward():
        mine = queries.at[:, :, me_k]
        pltpu.make_async_copy(mine, mine, q_recv).wait()
        for step in range(planes):
            for half, g in enumerate(groups(step)):
                slots = queries.at[g, half, me_k]
                pltpu.make_async_remote_copy(
                    src_ref=slots, dst_ref=slots, send_sem=f_send, recv_sem=f_recv.at[g * 2 + half],
                    device_id=sibling, device_id_type=MESH,
                ).start()

    def forwarded(step):
        for half, g in enumerate(groups(step)):
            slots = queries.at[g, half, 1 - me_k]
            pltpu.make_async_copy(slots, slots, f_recv.at[g * 2 + half]).wait()

    project(0, 0)
    pl.semaphore_wait(barrier, chips - 1 + planes)
    send_along_z()
    project(1, 0)
    send_in_plane()
    lax.fori_loop(2, rows // tile, project, 0)
    forward()
    forwarded(0)

    step_rows = near * lat_rows
    units = [(half, j) for half in range(2) for j in range(2)]
    chunk, part_rows = 256, 1024
    last = 2 * planes - 1
    block = own.shape[1:]
    flat = (block[0] * block[1] * block[2], block[3])

    def where_at(it):
        return lax.div(it, 2), lax.rem(me_k + 1 + it, 2)

    def load_query(it, unit):
        half, j = unit
        step, k = where_at(it)
        g = groups(step)[half]
        q = queries[g, half, k, :, :, j * 128:(j + 1) * 128].reshape(step_rows, 128)
        zero = jnp.zeros_like(q)
        return jnp.concatenate([jnp.where(low, q, zero), jnp.where(low, zero, q)], 0), g * 2 + j, half * 2 + k

    def score(u, q, pair, tile_at, at, peak):
        s = lax.dot_general(q, keys[pair, at, :], (((1,), (1,)), ((), ())), preferred_element_type=F32)
        off = bias[tile_at, :, at]
        s = jnp.concatenate([s[:step_rows] + off, s[step_rows:] + off], 0)
        scores[u % 2, :, at] = s
        for i in range(chunk // 128):
            piece = s[:, i * 128:(i + 1) * 128]
            peak = piece if peak is None else jnp.maximum(peak, piece)
        return peak

    def top_of(peak):
        return jnp.broadcast_to(jnp.max(peak, axis=1, keepdims=True), peak.shape)

    peak = None
    loaded = load_query(0, units[0])
    for c in range(rows // chunk):
        peak = score(0, *loaded, pl.ds(c * chunk, chunk), peak)
    tops[...] = top_of(peak)

    def iteration(it, carry):
        step, _ = where_at(it)
        odd = lax.rem(it, 2)
        more = step < planes - 1

        @pl.when((odd == 1) & more)
        def _():
            forwarded(step + 1)

        here = groups(step)
        top = tops[...]
        stats = None
        for u in range(len(units)):
            nxt = u + 1
            if nxt < len(units):
                loaded = load_query(it, units[nxt])
            else:
                loaded = load_query(jnp.minimum(it + 1, last), units[0])
            half, j = units[u]
            peak = total = None
            for c in range(rows // chunk):
                at = pl.ds(c * chunk, chunk)
                peak = score(nxt, *loaded, at, peak)
                wide_top = jnp.concatenate([top] * (chunk // 128), 1)
                weights[:, at] = jnp.exp(scores[u % 2, :, at] - wide_top).astype(BF16)
                if (c + 1) * chunk % part_rows == 0:
                    at = pl.ds((c + 1) * chunk - part_rows, part_rows)
                    part = dot(weights[:, at], values[here[half] * 2 + j, at, :])
                    total = part if total is None else total + part
            both = jnp.where(low, total[:step_rows, :128], total[step_rows:, :128]).astype(BF16)
            own[it, half, :, :, j * 128:(j + 1) * 128] = both.reshape(near, lat_rows, 128)
            new = totals_of(lane, 2 * j, top[:step_rows], total[:step_rows, 128:])
            new = new + totals_of(lane, 2 * j + 1, top[step_rows:], total[step_rows:, 128:])
            if j == 0:
                stats = new
            else:
                own[it, half, :, :, 256:384] = (stats + new).astype(BF16).reshape(near, lat_rows, 128)
            top = top_of(peak)
        tops[...] = top

        @pl.when(odd == 0)
        def _():
            pltpu.make_async_remote_copy(
                src_ref=own.at[it], dst_ref=other.at[step], send_sem=o_send, recv_sem=o_recv.at[step],
                device_id=sibling, device_id_type=MESH,
            ).start()

        @pl.when((odd == 1) & more)
        def _():
            pltpu.make_async_copy(other.at[step], other.at[step], o_recv.at[step]).wait()
            merged[step] = merge([own[it].reshape(flat), other[step].reshape(flat)]).reshape(block)
            for half, g in enumerate(here):
                pltpu.make_async_remote_copy(
                    src_ref=merged.at[step, half], dst_ref=along_z.at[step, half],
                    send_sem=z_send, recv_sem=z_recv.at[step], device_id=(me_c, g), device_id_type=MESH,
                ).start()

        return carry

    lax.fori_loop(0, last + 1, iteration, 0)

    final = planes - 1
    pltpu.make_async_copy(other.at[final], other.at[final], o_recv.at[final]).wait()
    for step in range(planes - 1):
        pltpu.make_async_copy(along_z.at[step], along_z.at[step], z_recv.at[step]).wait()
    blocks = [own[last], other[final]] + [along_z[step] for step in range(planes - 1)]
    merged[final] = merge([one.reshape(flat) for one in blocks]).reshape(block)

    def send_part(away, carry):
        chip = lax.rem(me_p + away, chips)
        pltpu.make_async_remote_copy(
            src_ref=merged.at[final, lax.div(chip, near), lax.rem(chip, near)], dst_ref=arrived.at[me_p],
            send_sem=p_send, recv_sem=p_recv, device_id=in_chip(away), device_id_type=MESH,
        ).start()
        return carry

    lax.fori_loop(1, chips, send_part, 0)
    pltpu.make_async_copy(merged.at[final, me_half, lax.rem(me_p, near)], arrived.at[me_p], p_recv).start()

    width = wq_ref.shape[1]
    mine = pl.ds(pl.multiple_of(me_h * width, width), width)
    self_key = dot(lat_n, wk[:, mine]).astype(BF16)
    self_value = dot(lat_n, wv[:, mine]).astype(BF16).astype(F32)
    prod = query.astype(F32) * self_key.astype(F32)
    self_score = pick_dot(prod, iota((width, 128), 0) // HD == iota((width, 128), 1) % (width // HD))

    pltpu.make_async_copy(arrived, arrived, p_recv).wait()
    out_ref[...] = combine(arrived, self_score, self_value)
    sent = plane_query.at[pl.ds(0, planes - 1)]
    pltpu.make_async_copy(sent, sent, s_send).wait()
    sent = values.at[0, pl.ds(0, (chips - 1) * planes * lat_rows)]
    pltpu.make_async_copy(sent, sent, q_send).wait()
    sent = queries.at[:, :, 0]
    pltpu.make_async_copy(sent, sent, f_send).wait()
    pltpu.make_async_copy(other, other, o_send).wait()
    pltpu.make_async_copy(along_z, along_z, z_send).wait()
    sent = arrived.at[pl.ds(0, chips - 1)]
    pltpu.make_async_copy(sent, sent, p_send).wait()


def per_device(prefix, keep_blocks, keep_count, latent_inputs, latent_pos, w_query, w_key, w_value):
    ctx_size, head_size = lax.axis_size("ctx"), lax.axis_size("head")
    rows, d = prefix.shape
    lat_rows, width = latent_inputs.shape[0], w_query.shape[1]
    latents, cols = lat_rows * ctx_size, width * head_size
    pairs = cols // 128
    near = ctx_size // 4
    wide = width + 128
    vmem = pl.BlockSpec(memory_space=pltpu.VMEM)
    hbm = pl.BlockSpec(memory_space=pl.ANY)
    dma = pltpu.SemaphoreType.DMA
    return pl.pallas_call(
        functools.partial(whole_kernel, (ctx_size, head_size)),
        in_specs=[vmem] * 5 + [hbm] * 3,
        out_specs=vmem,
        out_shape=jax.ShapeDtypeStruct((lat_rows, width), BF16),
        scratch_shapes=[
            pltpu.VMEM((rows, d), BF16),
            pltpu.VMEM((d, cols), BF16),
            pltpu.VMEM((d, cols), BF16),
            pltpu.VMEM((pairs, rows, 128), BF16),
            pltpu.VMEM((pairs, rows, 256), BF16),
            pltpu.VMEM((head_size, 2, 2, near, lat_rows, width), BF16),
            pltpu.VMEM((head_size, lat_rows, width), BF16),
            pltpu.VMEM((4, latents // 4, rows), F32),
            pltpu.VMEM((2, 256, rows), F32),
            pltpu.VMEM((256, rows), BF16),
            pltpu.VMEM((256, 128), F32),
            pltpu.VMEM((2 * head_size, 2, near, lat_rows, wide), BF16),
            pltpu.VMEM((head_size, 2, near, lat_rows, wide), BF16),
            pltpu.VMEM((head_size, 2, near, lat_rows, wide), BF16),
            pltpu.VMEM((head_size - 1, 2, near, lat_rows, wide), BF16),
            pltpu.VMEM((ctx_size // 2, lat_rows, wide), BF16),
            dma((rows // 512,)),
            dma((2,)),
            dma,
            dma,
            dma,
            dma,
            dma,
            dma((2 * head_size,)),
            dma,
            dma((head_size,)),
            dma,
            dma((head_size - 1,)),
            dma,
            dma,
        ],
        name="whole",
        compiler_params=pltpu.CompilerParams(
            collective_id=0, has_side_effects=True, vmem_limit_bytes=60 << 20
        ),
        cost_estimate=pl.CostEstimate(
            flops=4 * rows * d * cols + 4 * latents * rows * cols,
            bytes_accessed=2 * rows * d + 4 * d * cols,
            transcendentals=latents * rows * 2 * pairs,
        ),
    )(
        latent_inputs, w_query, latent_pos.reshape(1, latents),
        keep_blocks.reshape(1, -1), keep_count.reshape(1, 1), prefix, w_key, w_value,
    )


def solution(mesh):
    return jax.shard_map(
        per_device,
        mesh=mesh,
        in_specs=(
            P(("ctx", "head"), None),
            P("head", "ctx", None),
            P("head", "ctx"),
            P("ctx", None),
            P(),
            P(None, "head"),
            P(),
            P(),
        ),
        out_specs=P("ctx", "head"),
        check_vma=False,
    )
```

```python
import functools

import jax
import jax.numpy as jnp
from jax import lax
from jax.experimental import pallas as pl
from jax.experimental.pallas import tpu as pltpu
from jax.sharding import PartitionSpec as P

HD = 64
BLOCK = 128
EPSILON = 1e-06
NEG_FILL = -1e30
FAR = 1 << 30
MESH = pl.DeviceIdType.MESH
F32, BF16 = jnp.float32, jnp.bfloat16


def normed(rows):
    wide = rows.astype(F32)
    factor = lax.rsqrt(jnp.mean(wide * wide, axis=-1, keepdims=True) + EPSILON)
    return (wide * factor).astype(BF16)


def dot(a, b):
    return jnp.dot(a, b, preferred_element_type=F32)


def pick_dot(x, ones):
    first = x.astype(BF16)
    rest = x - first.astype(F32)
    second = rest.astype(BF16)
    third = (rest - second.astype(F32)).astype(BF16)
    ones = ones.astype(BF16)
    return dot(first, ones) + dot(second, ones) + dot(third, ones)


def iota(shape, dim):
    return lax.broadcasted_iota(jnp.int32, shape, dim)


def split_two(x):
    high = x.astype(BF16).astype(F32)
    return high, x - high


def spread(value):
    high, rest = split_two(value)
    lane = iota((1, 128), 1)
    pieces = jnp.where(lane < 4, high, jnp.where(lane < 8, rest, 0.0)).astype(BF16)
    r, c = iota((128, 256), 0), iota((128, 256), 1)
    return dot(pieces, ((r < 8) & (r % 4 == c // HD)).astype(BF16))


def read_totals(stats):
    r, c = iota((128, 256), 0), iota((128, 256), 1)
    piece = jnp.where(c < 128, (r < 12).astype(jnp.int32), ((r >= 12) & (r < 20)).astype(jnp.int32))
    both = dot(stats, ((piece == 1) & (r % 4 == c % 4)).astype(BF16))
    return both[:, :128], both[:, 128:]


def combine(parts_ref, own, self_value):
    shards, rows, wide = parts_ref.shape
    parts = parts_ref[...]
    tops, sums = read_totals(parts[:, :, 256:].reshape(shards * rows, 128))
    tops = tops.reshape(shards, rows, 128)
    top = jnp.maximum(jnp.max(tops, axis=0), own)
    scale = jnp.exp(tops - top[None])
    self_weight = jnp.exp(own - top)
    denominator = jnp.sum(scale * sums.reshape(shards, rows, 128), axis=0) + self_weight
    wanted = jnp.concatenate([scale.reshape(shards * rows, 128), self_weight, 1.0 / denominator], 0)
    spreads = spread(wanted)
    scales = spreads[: shards * rows].reshape(shards, rows, 256)
    numerator = jnp.sum(scales * parts[:, :, :256].astype(F32), axis=0)
    numerator = numerator + spreads[shards * rows : shards * rows + rows] * self_value
    return (numerator * spreads[shards * rows + rows :]).astype(BF16)


def pieces_of(lane, top, weight_sum):
    t1, rest = split_two(top)
    t2, t3 = split_two(rest)
    s1, s2 = split_two(weight_sum)
    piece = jnp.where(lane < 4, t1, jnp.where(lane < 8, t2, jnp.where(lane < 12, t3, jnp.where(lane < 16, s1, s2))))
    return jnp.where(lane < 20, piece, 0.0)


def totals_of(lane, head, top, weight_sum):
    return jnp.where(lane % 4 == head, pieces_of(lane, top, weight_sum), 0.0)


def merge(blocks):
    rows = blocks[0].shape[0]
    many = jnp.concatenate(blocks, 0)
    cut = lambda whole: [whole[i * rows:(i + 1) * rows] for i in range(len(blocks))]
    tops, sums = read_totals(many[:, 256:])
    top = functools.reduce(jnp.maximum, cut(tops))
    scale = jnp.exp(tops - jnp.concatenate([top] * len(blocks), 0))
    total = sum(cut(many[:, :256].astype(F32) * spread(scale)))
    stats = pieces_of(iota((1, 128), 1), top, sum(cut(scale * sums)))
    return jnp.concatenate([total, stats], 1).astype(BF16)


def whole_kernel(
    sizes, lat_ref, wq_ref, lpos_ref, kb_ref, kc_ref, x_hbm, wk_hbm, wv_hbm, out_ref,
    x, wk, wv, keys, values, queries, plane_query, bias, scores, weights, tops, own, other, merged, along_z, arrived,
    x_sem, w_sem, s_send, s_recv, q_send, q_recv, f_send, f_recv, o_send, o_recv, z_send, z_recv, p_send, p_recv,
):
    ctx_size, planes = sizes
    chips = ctx_size // 2
    near = chips // 2
    me_c, me_h = lax.axis_index("ctx"), lax.axis_index("head")
    me_p, me_k = lax.div(me_c, 2), lax.rem(me_c, 2)
    me_half = lax.div(me_p, near)
    sibling = (me_p * 2 + 1 - me_k, me_h)
    rows = x.shape[0]
    tile = 512

    def x_copy(t):
        at = pl.ds(pl.multiple_of(t * tile, tile), tile)
        return pltpu.make_async_copy(x_hbm.at[at], x.at[at], x_sem.at[t])

    wk_copy = pltpu.make_async_copy(wk_hbm, wk, w_sem.at[0])
    wv_copy = pltpu.make_async_copy(wv_hbm, wv, w_sem.at[1])
    wk_copy.start()
    x_copy(0).start()
    wv_copy.start()
    for t in range(1, rows // tile):
        x_copy(t).start()

    barrier = pltpu.get_barrier_semaphore()

    def in_plane(away):
        return (me_c, lax.rem(me_h + away, planes))

    def in_chip(away):
        return (lax.rem(me_p + away, chips) * 2 + me_k, me_h)

    def greet(device):
        pl.semaphore_signal(barrier, inc=1, device_id=device, device_id_type=MESH)

    for away in range(1, planes):
        greet(in_plane(away))
    greet(sibling)

    def greet_chip(away, carry):
        greet(in_chip(away))
        return carry

    lax.fori_loop(1, chips, greet_chip, 0)

    lat_n = normed(lat_ref[...])
    query = (dot(lat_n, wq_ref[...]) * HD ** (-0.5)).astype(BF16)
    plane_query[me_h] = query
    lat_rows = lat_ref.shape[0]
    lane = iota((1, 128), 1)
    low = lane < HD

    first_pos = (me_c * planes + me_h) * rows
    for half in range(2):
        span = near * 2 * lat_rows
        at = pl.ds(half * span, span)
        pos = jnp.transpose(jnp.broadcast_to(lpos_ref[:, at], (128, span))).reshape(near, 2, lat_rows, 128)
        for k in range(2):
            pos_k = pos[:, k].reshape(near * lat_rows, 128)
            for b in range(rows // BLOCK):
                hit = (kb_ref[...] == b) & (iota(kb_ref.shape, 1) < kc_ref[...])
                kept = jnp.max(jnp.where(hit, 1.0, 0.0), axis=1, keepdims=True)
                at_b = pl.ds(b * BLOCK, BLOCK)
                key_pos = jnp.where(kept > 0.5, first_pos + b * BLOCK + lane, FAR)
                bias[half * 2 + k, :, at_b] = jnp.where(key_pos < pos_k, 0.0, NEG_FILL)
    values[:, :, 128:] = jnp.ones(values.shape[:2] + (128,), BF16)

    wk_copy.wait()
    wv_copy.wait()
    pairs = keys.shape[0]

    def project(t, carry):
        x_copy(t).wait()
        at = pl.ds(pl.multiple_of(t * tile, tile), tile)
        n = normed(x[at, :])
        k = dot(n, wk[...]).astype(BF16)
        for p in range(pairs):
            keys[p, at, :] = k[:, p * 128:(p + 1) * 128]
        v = dot(n, wv[...]).astype(BF16)
        for p in range(pairs):
            values[p, at, 0:128] = v[:, p * 128:(p + 1) * 128]
        return carry

    def groups(step):
        return lax.rem(me_h + 1 + step, planes), lax.rem(me_h + 2 * planes - 1 - step, planes)

    def send_along_z():
        for away in range(1, planes):
            mine = plane_query.at[me_h]
            pltpu.make_async_remote_copy(
                src_ref=mine, dst_ref=mine, send_sem=s_send, recv_sem=s_recv,
                device_id=in_plane(away), device_id_type=MESH,
            ).start()

    def send_in_plane():
        some = plane_query.at[pl.ds(0, planes - 1)]
        pltpu.make_async_copy(some, some, s_recv).wait()
        slots = queries.at[:, me_half, me_k, lax.rem(me_p, near)]

        def send(away, carry):
            pltpu.make_async_remote_copy(
                src_ref=plane_query, dst_ref=slots, send_sem=q_send, recv_sem=q_recv,
                device_id=in_chip(away), device_id_type=MESH,
            ).start()
            return carry

        lax.fori_loop(1, chips, send, 0)
        pltpu.make_async_copy(plane_query, slots, q_recv).start()

    def forward():
        mine = queries.at[:, :, me_k]
        pltpu.make_async_copy(mine, mine, q_recv).wait()
        for step in range(planes):
            for half, g in enumerate(groups(step)):
                slots = queries.at[g, half, me_k]
                pltpu.make_async_remote_copy(
                    src_ref=slots, dst_ref=slots, send_sem=f_send, recv_sem=f_recv.at[g * 2 + half],
                    device_id=sibling, device_id_type=MESH,
                ).start()

    def forwarded(step):
        for half, g in enumerate(groups(step)):
            slots = queries.at[g, half, 1 - me_k]
            pltpu.make_async_copy(slots, slots, f_recv.at[g * 2 + half]).wait()

    pl.semaphore_wait(barrier, chips - 1 + planes)
    send_along_z()
    project(0, 0)
    send_in_plane()
    lax.fori_loop(1, rows // tile, project, 0)
    forward()
    forwarded(0)

    step_rows = near * lat_rows
    units = [(half, j) for half in range(2) for j in range(2)]
    chunk, part_rows = 256, 1024
    last = 2 * planes - 1
    block = own.shape[1:]
    flat = (block[0] * block[1] * block[2], block[3])

    def where_at(it):
        return lax.div(it, 2), lax.rem(me_k + 1 + it, 2)

    def load_query(it, unit):
        half, j = unit
        step, k = where_at(it)
        g = groups(step)[half]
        q = queries[g, half, k, :, :, j * 128:(j + 1) * 128].reshape(step_rows, 128)
        zero = jnp.zeros_like(q)
        return jnp.concatenate([jnp.where(low, q, zero), jnp.where(low, zero, q)], 0), g * 2 + j, half * 2 + k

    def score(u, q, pair, tile_at, at, peak):
        s = lax.dot_general(q, keys[pair, at, :], (((1,), (1,)), ((), ())), preferred_element_type=F32)
        off = bias[tile_at, :, at]
        s = jnp.concatenate([s[:step_rows] + off, s[step_rows:] + off], 0)
        scores[u % 2, :, at] = s
        for i in range(chunk // 128):
            piece = s[:, i * 128:(i + 1) * 128]
            peak = piece if peak is None else jnp.maximum(peak, piece)
        return peak

    def top_of(peak):
        return jnp.broadcast_to(jnp.max(peak, axis=1, keepdims=True), peak.shape)

    peak = None
    loaded = load_query(0, units[0])
    for c in range(rows // chunk):
        peak = score(0, *loaded, pl.ds(c * chunk, chunk), peak)
    tops[...] = top_of(peak)

    def iteration(it, carry):
        step, _ = where_at(it)
        odd = lax.rem(it, 2)
        more = step < planes - 1

        @pl.when((odd == 1) & more)
        def _():
            forwarded(step + 1)

        here = groups(step)
        top = tops[...]
        stats = None
        for u in range(len(units)):
            nxt = u + 1
            if nxt < len(units):
                loaded = load_query(it, units[nxt])
            else:
                loaded = load_query(jnp.minimum(it + 1, last), units[0])
            half, j = units[u]
            peak = total = None
            for c in range(rows // chunk):
                at = pl.ds(c * chunk, chunk)
                peak = score(nxt, *loaded, at, peak)
                wide_top = jnp.concatenate([top] * (chunk // 128), 1)
                weights[:, at] = jnp.exp(scores[u % 2, :, at] - wide_top).astype(BF16)
                if (c + 1) * chunk % part_rows == 0:
                    at = pl.ds((c + 1) * chunk - part_rows, part_rows)
                    part = dot(weights[:, at], values[here[half] * 2 + j, at, :])
                    total = part if total is None else total + part
            both = jnp.where(low, total[:step_rows, :128], total[step_rows:, :128]).astype(BF16)
            own[it, half, :, :, j * 128:(j + 1) * 128] = both.reshape(near, lat_rows, 128)
            new = totals_of(lane, 2 * j, top[:step_rows], total[:step_rows, 128:])
            new = new + totals_of(lane, 2 * j + 1, top[step_rows:], total[step_rows:, 128:])
            if j == 0:
                stats = new
            else:
                own[it, half, :, :, 256:384] = (stats + new).astype(BF16).reshape(near, lat_rows, 128)
            top = top_of(peak)
        tops[...] = top

        @pl.when(odd == 0)
        def _():
            pltpu.make_async_remote_copy(
                src_ref=own.at[it], dst_ref=other.at[step], send_sem=o_send, recv_sem=o_recv.at[step],
                device_id=sibling, device_id_type=MESH,
            ).start()

        @pl.when((odd == 1) & more)
        def _():
            pltpu.make_async_copy(other.at[step], other.at[step], o_recv.at[step]).wait()
            merged[step] = merge([own[it].reshape(flat), other[step].reshape(flat)]).reshape(block)
            for half, g in enumerate(here):
                pltpu.make_async_remote_copy(
                    src_ref=merged.at[step, half], dst_ref=along_z.at[step, half],
                    send_sem=z_send, recv_sem=z_recv.at[step], device_id=(me_c, g), device_id_type=MESH,
                ).start()

        return carry

    lax.fori_loop(0, last + 1, iteration, 0)

    final = planes - 1
    pltpu.make_async_copy(other.at[final], other.at[final], o_recv.at[final]).wait()
    for step in range(planes - 1):
        pltpu.make_async_copy(along_z.at[step], along_z.at[step], z_recv.at[step]).wait()
    blocks = [own[last], other[final]] + [along_z[step] for step in range(planes - 1)]
    merged[final] = merge([one.reshape(flat) for one in blocks]).reshape(block)

    def send_part(away, carry):
        chip = lax.rem(me_p + away, chips)
        pltpu.make_async_remote_copy(
            src_ref=merged.at[final, lax.div(chip, near), lax.rem(chip, near)], dst_ref=arrived.at[me_p],
            send_sem=p_send, recv_sem=p_recv, device_id=in_chip(away), device_id_type=MESH,
        ).start()
        return carry

    lax.fori_loop(1, chips, send_part, 0)
    pltpu.make_async_copy(merged.at[final, me_half, lax.rem(me_p, near)], arrived.at[me_p], p_recv).start()

    width = wq_ref.shape[1]
    mine = pl.ds(pl.multiple_of(me_h * width, width), width)
    self_key = dot(lat_n, wk[:, mine]).astype(BF16)
    self_value = dot(lat_n, wv[:, mine]).astype(BF16).astype(F32)
    prod = query.astype(F32) * self_key.astype(F32)
    self_score = pick_dot(prod, iota((width, 128), 0) // HD == iota((width, 128), 1) % (width // HD))

    pltpu.make_async_copy(arrived, arrived, p_recv).wait()
    out_ref[...] = combine(arrived, self_score, self_value)
    sent = plane_query.at[pl.ds(0, planes - 1)]
    pltpu.make_async_copy(sent, sent, s_send).wait()
    sent = values.at[0, pl.ds(0, (chips - 1) * planes * lat_rows)]
    pltpu.make_async_copy(sent, sent, q_send).wait()
    sent = queries.at[:, :, 0]
    pltpu.make_async_copy(sent, sent, f_send).wait()
    pltpu.make_async_copy(other, other, o_send).wait()
    pltpu.make_async_copy(along_z, along_z, z_send).wait()
    sent = arrived.at[pl.ds(0, chips - 1)]
    pltpu.make_async_copy(sent, sent, p_send).wait()


def per_device(prefix, keep_blocks, keep_count, latent_inputs, latent_pos, w_query, w_key, w_value):
    ctx_size, head_size = lax.axis_size("ctx"), lax.axis_size("head")
    rows, d = prefix.shape
    lat_rows, width = latent_inputs.shape[0], w_query.shape[1]
    latents, cols = lat_rows * ctx_size, width * head_size
    pairs = cols // 128
    near = ctx_size // 4
    wide = width + 128
    vmem = pl.BlockSpec(memory_space=pltpu.VMEM)
    hbm = pl.BlockSpec(memory_space=pl.ANY)
    dma = pltpu.SemaphoreType.DMA
    return pl.pallas_call(
        functools.partial(whole_kernel, (ctx_size, head_size)),
        in_specs=[vmem] * 5 + [hbm] * 3,
        out_specs=vmem,
        out_shape=jax.ShapeDtypeStruct((lat_rows, width), BF16),
        scratch_shapes=[
            pltpu.VMEM((rows, d), BF16),
            pltpu.VMEM((d, cols), BF16),
            pltpu.VMEM((d, cols), BF16),
            pltpu.VMEM((pairs, rows, 128), BF16),
            pltpu.VMEM((pairs, rows, 256), BF16),
            pltpu.VMEM((head_size, 2, 2, near, lat_rows, width), BF16),
            pltpu.VMEM((head_size, lat_rows, width), BF16),
            pltpu.VMEM((4, latents // 4, rows), F32),
            pltpu.VMEM((2, 256, rows), F32),
            pltpu.VMEM((256, rows), BF16),
            pltpu.VMEM((256, 128), F32),
            pltpu.VMEM((2 * head_size, 2, near, lat_rows, wide), BF16),
            pltpu.VMEM((head_size, 2, near, lat_rows, wide), BF16),
            pltpu.VMEM((head_size, 2, near, lat_rows, wide), BF16),
            pltpu.VMEM((head_size - 1, 2, near, lat_rows, wide), BF16),
            pltpu.VMEM((ctx_size // 2, lat_rows, wide), BF16),
            dma((rows // 512,)),
            dma((2,)),
            dma,
            dma,
            dma,
            dma,
            dma,
            dma((2 * head_size,)),
            dma,
            dma((head_size,)),
            dma,
            dma((head_size - 1,)),
            dma,
            dma,
        ],
        name="whole",
        compiler_params=pltpu.CompilerParams(
            collective_id=0, has_side_effects=True, vmem_limit_bytes=60 << 20
        ),
        cost_estimate=pl.CostEstimate(
            flops=4 * rows * d * cols + 4 * latents * rows * cols,
            bytes_accessed=2 * rows * d + 4 * d * cols,
            transcendentals=latents * rows * 2 * pairs,
        ),
    )(
        latent_inputs, w_query, latent_pos.reshape(1, latents),
        keep_blocks.reshape(1, -1), keep_count.reshape(1, 1), prefix, w_key, w_value,
    )


def solution(mesh):
    return jax.shard_map(
        per_device,
        mesh=mesh,
        in_specs=(
            P(("ctx", "head"), None),
            P("head", "ctx", None),
            P("head", "ctx"),
            P("ctx", None),
            P(),
            P(None, "head"),
            P(),
            P(),
        ),
        out_specs=P("ctx", "head"),
        check_vma=False,
    )
```

```python
import functools

import jax
import jax.numpy as jnp
from jax import lax
from jax.experimental import pallas as pl
from jax.experimental.pallas import tpu as pltpu
from jax.sharding import PartitionSpec as P

HD = 64
BLOCK = 128
EPSILON = 1e-06
NEG_FILL = -1e30
FAR = 1 << 30
MESH = pl.DeviceIdType.MESH
F32, BF16 = jnp.float32, jnp.bfloat16


def normed(rows):
    wide = rows.astype(F32)
    factor = lax.rsqrt(jnp.mean(wide * wide, axis=-1, keepdims=True) + EPSILON)
    return (wide * factor).astype(BF16)


def dot(a, b):
    return jnp.dot(a, b, preferred_element_type=F32)


def pick_dot(x, ones):
    first = x.astype(BF16)
    rest = x - first.astype(F32)
    second = rest.astype(BF16)
    third = (rest - second.astype(F32)).astype(BF16)
    ones = ones.astype(BF16)
    return dot(first, ones) + dot(second, ones) + dot(third, ones)


def iota(shape, dim):
    return lax.broadcasted_iota(jnp.int32, shape, dim)


def split_two(x):
    high = x.astype(BF16).astype(F32)
    return high, x - high


def spread(value):
    high, rest = split_two(value)
    lane = iota((1, 128), 1)
    pieces = jnp.where(lane < 4, high, jnp.where(lane < 8, rest, 0.0)).astype(BF16)
    r, c = iota((128, 256), 0), iota((128, 256), 1)
    return dot(pieces, ((r < 8) & (r % 4 == c // HD)).astype(BF16))


def read_totals(stats):
    r, c = iota((128, 256), 0), iota((128, 256), 1)
    piece = jnp.where(c < 128, (r < 12).astype(jnp.int32), ((r >= 12) & (r < 20)).astype(jnp.int32))
    both = dot(stats, ((piece == 1) & (r % 4 == c % 4)).astype(BF16))
    return both[:, :128], both[:, 128:]


def combine(parts_ref, own, self_value):
    shards, rows, wide = parts_ref.shape
    parts = parts_ref[...]
    tops, sums = read_totals(parts[:, :, 256:].reshape(shards * rows, 128))
    tops = tops.reshape(shards, rows, 128)
    top = jnp.maximum(jnp.max(tops, axis=0), own)
    scale = jnp.exp(tops - top[None])
    self_weight = jnp.exp(own - top)
    denominator = jnp.sum(scale * sums.reshape(shards, rows, 128), axis=0) + self_weight
    wanted = jnp.concatenate([scale.reshape(shards * rows, 128), self_weight, 1.0 / denominator], 0)
    spreads = spread(wanted)
    scales = spreads[: shards * rows].reshape(shards, rows, 256)
    numerator = jnp.sum(scales * parts[:, :, :256].astype(F32), axis=0)
    numerator = numerator + spreads[shards * rows : shards * rows + rows] * self_value
    return (numerator * spreads[shards * rows + rows :]).astype(BF16)


def pieces_of(lane, top, weight_sum):
    t1, rest = split_two(top)
    t2, t3 = split_two(rest)
    s1, s2 = split_two(weight_sum)
    piece = jnp.where(lane < 4, t1, jnp.where(lane < 8, t2, jnp.where(lane < 12, t3, jnp.where(lane < 16, s1, s2))))
    return jnp.where(lane < 20, piece, 0.0)


def totals_of(lane, head, top, weight_sum):
    return jnp.where(lane % 4 == head, pieces_of(lane, top, weight_sum), 0.0)


def merge(blocks):
    rows = blocks[0].shape[0]
    many = jnp.concatenate(blocks, 0)
    cut = lambda whole: [whole[i * rows:(i + 1) * rows] for i in range(len(blocks))]
    tops, sums = read_totals(many[:, 256:])
    top = functools.reduce(jnp.maximum, cut(tops))
    scale = jnp.exp(tops - jnp.concatenate([top] * len(blocks), 0))
    total = sum(cut(many[:, :256].astype(F32) * spread(scale)))
    stats = pieces_of(iota((1, 128), 1), top, sum(cut(scale * sums)))
    return jnp.concatenate([total, stats], 1).astype(BF16)


def whole_kernel(
    sizes, lat_ref, wq_ref, lpos_ref, kb_ref, kc_ref, x_hbm, wk_hbm, wv_hbm, out_ref,
    x, wk, wv, keys, values, queries, plane_query, bias, scores, weights, tops, own, other, merged, along_z, arrived,
    x_sem, w_sem, s_send, s_recv, q_send, q_recv, f_send, f_recv, o_send, o_recv, z_send, z_recv, p_send, p_recv,
):
    ctx_size, planes = sizes
    chips = ctx_size // 2
    near = chips // 2
    me_c, me_h = lax.axis_index("ctx"), lax.axis_index("head")
    me_p, me_k = lax.div(me_c, 2), lax.rem(me_c, 2)
    me_half = lax.div(me_p, near)
    sibling = (me_p * 2 + 1 - me_k, me_h)
    rows = x.shape[0]
    tile = 512

    def x_copy(t):
        at = pl.ds(pl.multiple_of(t * tile, tile), tile)
        return pltpu.make_async_copy(x_hbm.at[at], x.at[at], x_sem.at[t])

    wk_copy = pltpu.make_async_copy(wk_hbm, wk, w_sem.at[0])
    wv_copy = pltpu.make_async_copy(wv_hbm, wv, w_sem.at[1])
    wk_copy.start()
    x_copy(0).start()
    wv_copy.start()
    for t in range(1, rows // tile):
        x_copy(t).start()

    barrier = pltpu.get_barrier_semaphore()

    def in_plane(away):
        return (me_c, lax.rem(me_h + away, planes))

    def in_chip(away):
        return (lax.rem(me_p + away, chips) * 2 + me_k, me_h)

    def greet(device):
        pl.semaphore_signal(barrier, inc=1, device_id=device, device_id_type=MESH)

    for away in range(1, planes):
        greet(in_plane(away))
    greet(sibling)

    def greet_chip(away, carry):
        greet(in_chip(away))
        return carry

    lax.fori_loop(1, chips, greet_chip, 0)

    lat_n = normed(lat_ref[...])
    query = (dot(lat_n, wq_ref[...]) * HD ** (-0.5)).astype(BF16)
    plane_query[me_h] = query
    lat_rows = lat_ref.shape[0]
    lane = iota((1, 128), 1)
    low = lane < HD

    first_pos = (me_c * planes + me_h) * rows
    for half in range(2):
        span = near * 2 * lat_rows
        at = pl.ds(half * span, span)
        pos = jnp.transpose(jnp.broadcast_to(lpos_ref[:, at], (128, span))).reshape(near, 2, lat_rows, 128)
        for k in range(2):
            pos_k = pos[:, k].reshape(near * lat_rows, 128)
            for b in range(rows // BLOCK):
                hit = (kb_ref[...] == b) & (iota(kb_ref.shape, 1) < kc_ref[...])
                kept = jnp.max(jnp.where(hit, 1.0, 0.0), axis=1, keepdims=True)
                at_b = pl.ds(b * BLOCK, BLOCK)
                key_pos = jnp.where(kept > 0.5, first_pos + b * BLOCK + lane, FAR)
                bias[half * 2 + k, :, at_b] = jnp.where(key_pos < pos_k, 0.0, NEG_FILL)
    values[:, :, 128:] = jnp.ones(values.shape[:2] + (128,), BF16)

    wk_copy.wait()
    wv_copy.wait()
    pairs = keys.shape[0]

    def project(t, carry):
        x_copy(t).wait()
        at = pl.ds(pl.multiple_of(t * tile, tile), tile)
        n = normed(x[at, :])
        k = dot(n, wk[...]).astype(BF16)
        for p in range(pairs):
            keys[p, at, :] = k[:, p * 128:(p + 1) * 128]
        v = dot(n, wv[...]).astype(BF16)
        for p in range(pairs):
            values[p, at, 0:128] = v[:, p * 128:(p + 1) * 128]
        return carry

    def groups(step):
        return lax.rem(me_h + 1 + step, planes), lax.rem(me_h + 2 * planes - 1 - step, planes)

    def send_along_z():
        for away in range(1, planes):
            mine = plane_query.at[me_h]
            pltpu.make_async_remote_copy(
                src_ref=mine, dst_ref=mine, send_sem=s_send, recv_sem=s_recv,
                device_id=in_plane(away), device_id_type=MESH,
            ).start()

    def send_in_plane():
        some = plane_query.at[pl.ds(0, planes - 1)]
        pltpu.make_async_copy(some, some, s_recv).wait()
        slots = queries.at[:, me_half, me_k, lax.rem(me_p, near)]

        def send(away, carry):
            pltpu.make_async_remote_copy(
                src_ref=plane_query, dst_ref=slots, send_sem=q_send, recv_sem=q_recv,
                device_id=in_chip(away), device_id_type=MESH,
            ).start()
            return carry

        for away in range(1, chips):
            send(away, 0)
        pltpu.make_async_copy(plane_query, slots, q_recv).start()

    def forward():
        mine = queries.at[:, :, me_k]
        pltpu.make_async_copy(mine, mine, q_recv).wait()
        for step in range(planes):
            for half, g in enumerate(groups(step)):
                slots = queries.at[g, half, me_k]
                pltpu.make_async_remote_copy(
                    src_ref=slots, dst_ref=slots, send_sem=f_send, recv_sem=f_recv.at[g * 2 + half],
                    device_id=sibling, device_id_type=MESH,
                ).start()

    def forwarded(step):
        for half, g in enumerate(groups(step)):
            slots = queries.at[g, half, 1 - me_k]
            pltpu.make_async_copy(slots, slots, f_recv.at[g * 2 + half]).wait()

    pl.semaphore_wait(barrier, chips - 1 + planes)
    send_along_z()
    project(0, 0)
    send_in_plane()
    lax.fori_loop(1, rows // tile, project, 0)
    forward()
    forwarded(0)

    step_rows = near * lat_rows
    units = [(half, j) for half in range(2) for j in range(2)]
    chunk, part_rows = 256, 1024
    last = 2 * planes - 1
    block = own.shape[1:]
    flat = (block[0] * block[1] * block[2], block[3])

    def where_at(it):
        return lax.div(it, 2), lax.rem(me_k + 1 + it, 2)

    def load_query(it, unit):
        half, j = unit
        step, k = where_at(it)
        g = groups(step)[half]
        q = queries[g, half, k, :, :, j * 128:(j + 1) * 128].reshape(step_rows, 128)
        zero = jnp.zeros_like(q)
        return jnp.concatenate([jnp.where(low, q, zero), jnp.where(low, zero, q)], 0), g * 2 + j, half * 2 + k

    def score(u, q, pair, tile_at, at, peak):
        s = lax.dot_general(q, keys[pair, at, :], (((1,), (1,)), ((), ())), preferred_element_type=F32)
        off = bias[tile_at, :, at]
        s = jnp.concatenate([s[:step_rows] + off, s[step_rows:] + off], 0)
        scores[u % 2, :, at] = s
        for i in range(chunk // 128):
            piece = s[:, i * 128:(i + 1) * 128]
            peak = piece if peak is None else jnp.maximum(peak, piece)
        return peak

    def top_of(peak):
        return jnp.broadcast_to(jnp.max(peak, axis=1, keepdims=True), peak.shape)

    peak = None
    loaded = load_query(0, units[0])
    for c in range(rows // chunk):
        peak = score(0, *loaded, pl.ds(c * chunk, chunk), peak)
    tops[...] = top_of(peak)

    def iteration(it, carry):
        step, _ = where_at(it)
        odd = lax.rem(it, 2)
        more = step < planes - 1

        @pl.when((odd == 1) & more)
        def _():
            forwarded(step + 1)

        here = groups(step)
        top = tops[...]
        stats = None
        for u in range(len(units)):
            nxt = u + 1
            if nxt < len(units):
                loaded = load_query(it, units[nxt])
            else:
                loaded = load_query(jnp.minimum(it + 1, last), units[0])
            half, j = units[u]
            peak = total = None
            for c in range(rows // chunk):
                at = pl.ds(c * chunk, chunk)
                peak = score(nxt, *loaded, at, peak)
                wide_top = jnp.concatenate([top] * (chunk // 128), 1)
                weights[:, at] = jnp.exp(scores[u % 2, :, at] - wide_top).astype(BF16)
                if (c + 1) * chunk % part_rows == 0:
                    at = pl.ds((c + 1) * chunk - part_rows, part_rows)
                    part = dot(weights[:, at], values[here[half] * 2 + j, at, :])
                    total = part if total is None else total + part
            both = jnp.where(low, total[:step_rows, :128], total[step_rows:, :128]).astype(BF16)
            own[it, half, :, :, j * 128:(j + 1) * 128] = both.reshape(near, lat_rows, 128)
            new = totals_of(lane, 2 * j, top[:step_rows], total[:step_rows, 128:])
            new = new + totals_of(lane, 2 * j + 1, top[step_rows:], total[step_rows:, 128:])
            if j == 0:
                stats = new
            else:
                own[it, half, :, :, 256:384] = (stats + new).astype(BF16).reshape(near, lat_rows, 128)
            top = top_of(peak)
        tops[...] = top

        @pl.when(odd == 0)
        def _():
            pltpu.make_async_remote_copy(
                src_ref=own.at[it], dst_ref=other.at[step], send_sem=o_send, recv_sem=o_recv.at[step],
                device_id=sibling, device_id_type=MESH,
            ).start()

        @pl.when((odd == 1) & more)
        def _():
            pltpu.make_async_copy(other.at[step], other.at[step], o_recv.at[step]).wait()
            merged[step] = merge([own[it].reshape(flat), other[step].reshape(flat)]).reshape(block)
            for half, g in enumerate(here):
                pltpu.make_async_remote_copy(
                    src_ref=merged.at[step, half], dst_ref=along_z.at[step, half],
                    send_sem=z_send, recv_sem=z_recv.at[step], device_id=(me_c, g), device_id_type=MESH,
                ).start()

        return carry

    lax.fori_loop(0, last + 1, iteration, 0)

    final = planes - 1
    pltpu.make_async_copy(other.at[final], other.at[final], o_recv.at[final]).wait()
    for step in range(planes - 1):
        pltpu.make_async_copy(along_z.at[step], along_z.at[step], z_recv.at[step]).wait()
    blocks = [own[last], other[final]] + [along_z[step] for step in range(planes - 1)]
    merged[final] = merge([one.reshape(flat) for one in blocks]).reshape(block)

    def send_part(away, carry):
        chip = lax.rem(me_p + away, chips)
        pltpu.make_async_remote_copy(
            src_ref=merged.at[final, lax.div(chip, near), lax.rem(chip, near)], dst_ref=arrived.at[me_p],
            send_sem=p_send, recv_sem=p_recv, device_id=in_chip(away), device_id_type=MESH,
        ).start()
        return carry

    for away in range(1, chips):
        send_part(away, 0)
    pltpu.make_async_copy(merged.at[final, me_half, lax.rem(me_p, near)], arrived.at[me_p], p_recv).start()

    width = wq_ref.shape[1]
    mine = pl.ds(pl.multiple_of(me_h * width, width), width)
    self_key = dot(lat_n, wk[:, mine]).astype(BF16)
    self_value = dot(lat_n, wv[:, mine]).astype(BF16).astype(F32)
    prod = query.astype(F32) * self_key.astype(F32)
    self_score = pick_dot(prod, iota((width, 128), 0) // HD == iota((width, 128), 1) % (width // HD))

    pltpu.make_async_copy(arrived, arrived, p_recv).wait()
    out_ref[...] = combine(arrived, self_score, self_value)
    sent = plane_query.at[pl.ds(0, planes - 1)]
    pltpu.make_async_copy(sent, sent, s_send).wait()
    sent = values.at[0, pl.ds(0, (chips - 1) * planes * lat_rows)]
    pltpu.make_async_copy(sent, sent, q_send).wait()
    sent = queries.at[:, :, 0]
    pltpu.make_async_copy(sent, sent, f_send).wait()
    pltpu.make_async_copy(other, other, o_send).wait()
    pltpu.make_async_copy(along_z, along_z, z_send).wait()
    sent = arrived.at[pl.ds(0, chips - 1)]
    pltpu.make_async_copy(sent, sent, p_send).wait()


def per_device(prefix, keep_blocks, keep_count, latent_inputs, latent_pos, w_query, w_key, w_value):
    ctx_size, head_size = lax.axis_size("ctx"), lax.axis_size("head")
    rows, d = prefix.shape
    lat_rows, width = latent_inputs.shape[0], w_query.shape[1]
    latents, cols = lat_rows * ctx_size, width * head_size
    pairs = cols // 128
    near = ctx_size // 4
    wide = width + 128
    vmem = pl.BlockSpec(memory_space=pltpu.VMEM)
    hbm = pl.BlockSpec(memory_space=pl.ANY)
    dma = pltpu.SemaphoreType.DMA
    return pl.pallas_call(
        functools.partial(whole_kernel, (ctx_size, head_size)),
        in_specs=[vmem] * 5 + [hbm] * 3,
        out_specs=vmem,
        out_shape=jax.ShapeDtypeStruct((lat_rows, width), BF16),
        scratch_shapes=[
            pltpu.VMEM((rows, d), BF16),
            pltpu.VMEM((d, cols), BF16),
            pltpu.VMEM((d, cols), BF16),
            pltpu.VMEM((pairs, rows, 128), BF16),
            pltpu.VMEM((pairs, rows, 256), BF16),
            pltpu.VMEM((head_size, 2, 2, near, lat_rows, width), BF16),
            pltpu.VMEM((head_size, lat_rows, width), BF16),
            pltpu.VMEM((4, latents // 4, rows), F32),
            pltpu.VMEM((2, 256, rows), F32),
            pltpu.VMEM((256, rows), BF16),
            pltpu.VMEM((256, 128), F32),
            pltpu.VMEM((2 * head_size, 2, near, lat_rows, wide), BF16),
            pltpu.VMEM((head_size, 2, near, lat_rows, wide), BF16),
            pltpu.VMEM((head_size, 2, near, lat_rows, wide), BF16),
            pltpu.VMEM((head_size - 1, 2, near, lat_rows, wide), BF16),
            pltpu.VMEM((ctx_size // 2, lat_rows, wide), BF16),
            dma((rows // 512,)),
            dma((2,)),
            dma,
            dma,
            dma,
            dma,
            dma,
            dma((2 * head_size,)),
            dma,
            dma((head_size,)),
            dma,
            dma((head_size - 1,)),
            dma,
            dma,
        ],
        name="whole",
        compiler_params=pltpu.CompilerParams(
            collective_id=0, has_side_effects=True, vmem_limit_bytes=60 << 20
        ),
        cost_estimate=pl.CostEstimate(
            flops=4 * rows * d * cols + 4 * latents * rows * cols,
            bytes_accessed=2 * rows * d + 4 * d * cols,
            transcendentals=latents * rows * 2 * pairs,
        ),
    )(
        latent_inputs, w_query, latent_pos.reshape(1, latents),
        keep_blocks.reshape(1, -1), keep_count.reshape(1, 1), prefix, w_key, w_value,
    )


def solution(mesh):
    return jax.shard_map(
        per_device,
        mesh=mesh,
        in_specs=(
            P(("ctx", "head"), None),
            P("head", "ctx", None),
            P("head", "ctx"),
            P("ctx", None),
            P(),
            P(None, "head"),
            P(),
            P(),
        ),
        out_specs=P("ctx", "head"),
        check_vma=False,
    )
```
